32 devices in a mesh: gx: 8 (over z, y), gy: 4 (over x, core).
Axes of the slice: x: 2, y: 2, z: 4, core: 2. Of those that a mesh axis runs over, the one named last changes fastest.
Arguments:
- forward_pops: float32 [19, 64, 64, 128], P(None, 'gx', 'gy'), may hold values from 0.005 to 1, as said below
- later_adjoint: float32 [19, 64, 64, 128], P(None, 'gx', 'gy'), may hold values from -6 to 6
- design: float32 [64, 64, 128], P('gx', 'gy'), may hold values from 0 to 1
- node_type: int32 [64, 64, 128], P('gx', 'gy'), may hold values from 0 to 4, as said below
- region: int32 [64, 64, 128], P('gx', 'gy'), may hold values from 0 to 7
Outputs:
- adjoint: float32 [19, 64, 64, 128], P(None, 'gx', 'gy')
- sensitivity: float32 [64, 64, 128], P('gx', 'gy')
- objective: float32 [], replicated
- volumes: float32 [8], replicated
The draws below stay inside these ranges and needn't reach their ends.
Inputs may be any that keep to these rules, and one draw needn't show every extreme that they name: `node_type`: 0 fluid, 1 design, 2 wall, 3 inlet, 4 outlet. `forward_pops`: positive populations.
All inputs are finite; a program needn't handle non-finite values.
Results may differ from the reference program's by a relative error of at most 0.00002.
Values sent between devices are 32-bit elements; how exact they have to be, the bound alone decides.
A program may use at most 64 MiB of HBM per device.

```python
import math
import jax
import jax.numpy as jnp

Q = 19
NZ = 128
RAD = 3
REG = 8
NX = 64
NY = 64


WEIGHT_LIST = [1.0 / 3.0] + [1.0 / 18.0] * 6 + [1.0 / 36.0] * 12


XDIR_LIST = [0.0, 1.0, -1.0, 0.0, 0.0, 0.0, 0.0, 1.0, -1.0, 1.0, -1.0, 1.0, -1.0, 1.0, -1.0, 0.0, 0.0, 0.0, 0.0]


def draw_forward_pops(key, part):
    table = jnp.array(WEIGHT_LIST, jnp.float32)[:, None, None, None]
    xdir = jnp.array(XDIR_LIST, jnp.float32)[:, None, None, None]
    spread_noise = jnp.exp(jax.random.uniform(key, (Q, NX, NY, NZ), jnp.float32, -0.5, 0.5))
    return table * (1.0 + 0.3 * xdir) * spread_noise


def draw_design(key, part):
    key_power = jax.random.fold_in(key, 11)
    key_base = jax.random.fold_in(key, 12)
    exponent = jnp.exp(jax.random.uniform(key_power, (NX, NY, 1), jnp.float32, math.log(0.3), math.log(3.0)))
    uniform_base = jax.random.uniform(key_base, (NX, NY, NZ), jnp.float32, 0.0, 1.0)
    return jnp.power(uniform_base, exponent)


def draw_node_type(key, part):
    draw_code = jax.random.randint(key, (NX, NY, NZ), 0, 16)
    return jnp.where(draw_code < 7, 0, jnp.where(draw_code < 13, 1, draw_code - 11)).astype(jnp.int32)


def place_ends(values, rng, low, largest):
    place = [jax.random.randint(jax.random.fold_in(rng, axis), (), 0, length) for axis, length in enumerate(values.shape)]
    main_axis = values.shape.index(max(values.shape))
    neighbour = place[:main_axis] + [(place[main_axis] + 1) % values.shape[main_axis]] + place[main_axis + 1:]
    return values.at[tuple(place)].set(low).at[tuple(neighbour)].set(largest)


def steps_of(key, shape, shards, least, top_value):
    def one(position, shards_of):
        steps = jax.random.uniform(jax.random.fold_in(jax.random.fold_in(key, 6), position), (shards_of,), jnp.float32, least / len(shards), top_value / len(shards))
        return jnp.repeat(jnp.exp(steps), shape[position] // shards_of).reshape((-1,) + (1,) * (len(shape) - position - 1))

    factor_of = one(*shards[0])
    for cut in shards[1:]:
        factor_of = factor_of * one(*cut)
    return factor_of


def noise(key, dims, deviation, reach, cuts=(), kind=jnp.bfloat16):
    level = steps_of(key, dims, cuts, -0.22, 0.18) if cuts else 1.0
    values = jax.random.normal(key, dims, jnp.float32) * deviation * level
    return jnp.minimum(jnp.maximum(values, -reach), reach).astype(kind)


def setup_inputs(seed: int = 0) -> dict:
    key_list = jax.random.split(jax.random.key(seed), 6)
    return {
        "forward_pops": draw_forward_pops(jax.random.fold_in(key_list[5], 71), 0),
        "later_adjoint": noise(key_list[1], (Q, NX, NY, NZ), 1.0, 6.0, ((1, 8), (2, 4)), jnp.float32),
        "design": draw_design(jax.random.fold_in(key_list[5], 71), 0),
        "node_type": draw_node_type(jax.random.fold_in(key_list[5], 71), 0),
        "region": place_ends(jax.random.randint(key_list[4], (NX, NY, NZ), 0, REG), jax.random.fold_in(key_list[4], 1), 0, REG - 1).astype(jnp.int32),
    }


VELOCITY = [(0, 0, 0), (1, 0, 0), (-1, 0, 0), (0, 1, 0), (0, -1, 0), (0, 0, 1), (0, 0, -1), (1, 1, 0), (-1, -1, 0), (1, -1, 0), (-1, 1, 0), (1, 0, 1), (-1, 0, -1), (1, 0, -1), (-1, 0, 1), (0, 1, 1), (0, -1, -1), (0, 1, -1), (0, -1, 1)]
WEIGHTS = [1.0 / 3.0] + [1.0 / 18.0] * 6 + [1.0 / 36.0] * 12
OPPOSITE = [0, 2, 1, 4, 3, 6, 5, 8, 7, 10, 9, 12, 11, 14, 13, 16, 15, 18, 17]
RELAXATION = 1.0 / 0.6
BRINKMAN = 0.9

def moments(populations):
    density = populations[0]
    for i in range(1, 19):
        density = density + populations[i]
    momenta = []
    for a in range(3):
        running = jnp.zeros_like(density)
        for i in range(19):
            if VELOCITY[i][a] == 1:
                running = running + populations[i]
            elif VELOCITY[i][a] == -1:
                running = running - populations[i]
        momenta.append(running)
    return (density, momenta)

def projections(velocity):
    result = []
    for i in range(19):
        running = jnp.zeros_like(velocity[0])
        for a in range(3):
            if VELOCITY[i][a] != 0:
                running = running + VELOCITY[i][a] * velocity[a]
        result.append(running)
    return result

def rates(kind):
    return jnp.where(kind <= 1, RELAXATION, 1.0)

def collide(populations, kind, factor):
    density, momenta = moments(populations)
    plain = [m / density for m in momenta]
    velocity = [factor * p for p in plain]
    speed_sq = velocity[0] * velocity[0] + velocity[1] * velocity[1] + velocity[2] * velocity[2]
    along = projections(velocity)
    omega_cell = rates(kind)
    wall = kind == 2
    output = []
    for i in range(19):
        balance = WEIGHTS[i] * density * (1.0 + 3.0 * along[i] + 4.5 * along[i] * along[i] - 1.5 * speed_sq)
        relaxed = (1.0 - omega_cell) * populations[i] + omega_cell * balance
        output.append(jnp.where(wall, populations[OPPOSITE[i]], relaxed))
    return jnp.stack(output)

def adjoint_collide(incoming, populations, kind, factor):
    density, momenta = moments(populations)
    plain = [m / density for m in momenta]
    velocity = [factor * p for p in plain]
    speed_sq = velocity[0] * velocity[0] + velocity[1] * velocity[1] + velocity[2] * velocity[2]
    along = projections(velocity)
    omega_cell = rates(kind)
    wall = kind == 2
    scalar_part = jnp.zeros_like(density)
    vector_part = [jnp.zeros_like(density), jnp.zeros_like(density), jnp.zeros_like(density)]
    for j in range(19):
        weighted = WEIGHTS[j] * incoming[j]
        scalar_part = scalar_part + weighted * (1.0 + 3.0 * along[j] + 4.5 * along[j] * along[j] - 1.5 * speed_sq)
        for a in range(3):
            vector_part[a] = vector_part[a] + weighted * (3.0 * VELOCITY[j][a] + 9.0 * along[j] * VELOCITY[j][a] - 3.0 * velocity[a])
    output = []
    for i in range(19):
        coupling = scalar_part
        for a in range(3):
            coupling = coupling + vector_part[a] * (factor * VELOCITY[i][a] - velocity[a])
        relaxed = (1.0 - omega_cell) * incoming[i] + omega_cell * coupling
        output.append(jnp.where(wall, incoming[OPPOSITE[i]], relaxed))
    inner = vector_part[0] * plain[0] + vector_part[1] * plain[1] + vector_part[2] * plain[2]
    gradient = jnp.where(wall, 0.0, omega_cell * density * inner)
    return (jnp.stack(output), gradient)

def displace(extended, sign):
    padded = jnp.pad(extended, ((0, 0), (0, 0), (0, 0), (1, 1)))
    span_x = extended.shape[1] - 2
    span_y = extended.shape[2] - 2
    span_z = extended.shape[3]
    pieces = []
    for i in range(19):
        off_x = 1 + sign * VELOCITY[i][0]
        off_y = 1 + sign * VELOCITY[i][1]
        off_z = 1 + sign * VELOCITY[i][2]
        pieces.append(padded[i, off_x:off_x + span_x, off_y:off_y + span_y, off_z:off_z + span_z])
    return jnp.stack(pieces)

def wrap_rim(populations):
    return jnp.pad(populations, ((0, 0), (1, 1), (1, 1), (0, 0)), mode='wrap')

def filter_taps(padded):
    span_x = padded.shape[0] - 2 * RAD
    span_y = padded.shape[1] - 2 * RAD
    span_z = padded.shape[2] - 2 * RAD
    running = jnp.zeros((span_x, span_y, span_z), jnp.float32)
    for a in range(-RAD, RAD + 1):
        for b in range(-RAD, RAD + 1):
            for c in range(-RAD, RAD + 1):
                weight = RAD + 1 - math.sqrt(a * a + b * b + c * c)
                if weight > 0:
                    running = running + weight * padded[RAD + a:RAD + a + span_x, RAD + b:RAD + b + span_y, RAD + c:RAD + c + span_z]
    return running

def filter_norm(depth):
    block = jnp.pad(jnp.ones((2 * RAD + 1, 2 * RAD + 1, depth), jnp.float32), ((0, 0), (0, 0), (RAD, RAD)))
    return filter_taps(block)

def density_filter(field):
    padded = jnp.pad(field, ((RAD, RAD), (RAD, RAD), (0, 0)), mode='wrap')
    return filter_taps(jnp.pad(padded, ((0, 0), (0, 0), (RAD, RAD))))

def reference(forward_pops, later_adjoint, design, node_type, region):
    norm_field = filter_norm(design.shape[2])
    filtered = density_filter(design) / norm_field
    factor = jnp.where(node_type == 1, 1.0 - BRINKMAN * (1.0 - filtered), 1.0)
    post = collide(forward_pops, node_type, factor)
    next_pops = displace(wrap_rim(post), -1)
    density, momenta = moments(next_pops)
    objective = jnp.sum(jnp.where(node_type == 4, momenta[0], 0.0))
    volumes = jnp.stack([jnp.sum(jnp.where((node_type == 1) & (region == r), filtered, 0.0)) for r in range(REG)])
    incoming = displace(wrap_rim(later_adjoint), 1)
    middle, first_grad = adjoint_collide(incoming, next_pops, node_type, factor)
    source = jnp.where(node_type == 4, 1.0, 0.0)
    middle = middle + jnp.stack([VELOCITY[i][0] * source for i in range(19)])
    incoming = displace(wrap_rim(middle), 1)
    adjoint, second_grad = adjoint_collide(incoming, forward_pops, node_type, factor)
    raw = jnp.where(node_type == 1, BRINKMAN * (first_grad + second_grad), 0.0) / norm_field
    sensitivity = density_filter(raw)
    return (adjoint, sensitivity, objective, volumes)
```

```python
import functools
import math

import jax
import jax.numpy as jnp
from jax import lax
from jax.experimental import pallas as pl
from jax.experimental.pallas import tpu as pltpu
from jax.sharding import PartitionSpec as P

RAD = 3
REG = 8
MESH = pl.DeviceIdType.MESH

VELOCITY = [
    (0, 0, 0),
    (1, 0, 0),
    (-1, 0, 0),
    (0, 1, 0),
    (0, -1, 0),
    (0, 0, 1),
    (0, 0, -1),
    (1, 1, 0),
    (-1, -1, 0),
    (1, -1, 0),
    (-1, 1, 0),
    (1, 0, 1),
    (-1, 0, -1),
    (1, 0, -1),
    (-1, 0, 1),
    (0, 1, 1),
    (0, -1, -1),
    (0, 1, -1),
    (0, -1, 1),
]
W0, W1, W2 = 1.0 / 3.0, 1.0 / 18.0, 1.0 / 36.0
PAIRS = [1, 3, 5, 7, 9, 11, 13, 15, 17]
OPPOSITE = [0, 2, 1, 4, 3, 6, 5, 8, 7, 10, 9, 12, 11, 14, 13, 16, 15, 18, 17]
RELAXATION = 1.0 / 0.6
BRINKMAN = 0.9

DIRS = [(1, 0), (-1, 0), (0, 1), (0, -1), (1, 1), (-1, -1), (1, -1), (-1, 1)]
ROWS = 8
POST, LATER, MIDDLE = 0, 1, 2
DESIGN, RAW = 3, 4


def weight(a, b, c):
    return max(RAD + 1 - math.sqrt(a * a + b * b + c * c), 0.0)


def crossing(direction, sign):
    return [
        i
        for i in range(19)
        if all(
            direction[a] == 0 or sign * VELOCITY[i][a] == direction[a] for a in range(2)
        )
    ]


def lanes(shape):
    return lax.broadcasted_iota(jnp.int32, shape, len(shape) - 1)


def shifted(value, offset):
    if offset == 0:
        return value
    depth = value.shape[-1]
    z = lanes(value.shape)
    rolled = pltpu.roll(value, (-offset) % depth, value.ndim - 1)
    inside = z < depth - offset if offset > 0 else z >= -offset
    return jnp.where(inside, rolled, 0.0)


def inverse_norm(shape):
    depth = shape[-1]
    z = lanes(shape)
    span = range(-RAD, RAD + 1)
    norm = jnp.zeros(shape, jnp.float32)
    for c in span:
        layer = sum(weight(a, b, c) for a in span for b in span)
        inside = (z + c >= 0) & (z + c < depth)
        norm = norm + jnp.where(inside, layer, 0.0)
    return 1.0 / norm


def filter_taps(field, x, y):
    classes = {}
    for a in range(-RAD, RAD + 1):
        for b in range(-RAD, RAD + 1):
            if weight(a, b, 0) > 0:
                value = field[x + RAD + a, ROWS + y + b : 2 * ROWS + y + b, :]
                key = a * a + b * b
                classes[key] = classes[key] + value if key in classes else value
    result = None
    for c in range(RAD + 1):
        layer = None
        for key, value in classes.items():
            w = max(RAD + 1 - math.sqrt(key + c * c), 0.0)
            if w > 0:
                layer = w * value if layer is None else layer + w * value
        if c == 0:
            result = layer
        else:
            result = result + shifted(layer, c) + shifted(layer, -c)
    return result


def pairs_of(p):
    return (
        {i: p[i] + p[i + 1] for i in PAIRS},
        {i: p[i] - p[i + 1] for i in PAIRS},
    )


def moments(p):
    even, odd = pairs_of(p)
    density = p[0] + (
        ((even[1] + even[3]) + (even[5] + even[7]))
        + ((even[9] + even[11]) + (even[13] + (even[15] + even[17])))
    )
    momenta = [
        (odd[1] + odd[7]) + (odd[9] + (odd[11] + odd[13])),
        (odd[3] + odd[7]) + (odd[15] + odd[17] - odd[9]),
        (odd[5] + odd[11]) + (odd[15] - odd[13] - odd[17]),
    ]
    return density, momenta


def along(i, u):
    total = None
    for a in range(3):
        if VELOCITY[i][a] != 0:
            if total is None:
                total = u[a]
            elif VELOCITY[i][a] > 0:
                total = total + u[a]
            else:
                total = total - u[a]
    return total


def rates(kind):
    return jnp.where(kind <= 1, RELAXATION, 1.0)


def collide(p, density, plain, kind, factor):
    u = [factor * v for v in plain]
    base = 1.0 - 1.5 * (u[0] * u[0] + u[1] * u[1] + u[2] * u[2])
    omega = rates(kind)
    keep = 1.0 - omega
    wall = kind == 2
    scale = omega * density
    scale1 = W1 * scale
    scale2 = W2 * scale
    out = [None] * 19
    out[0] = jnp.where(wall, p[0], keep * p[0] + (W0 * scale) * base)
    for i in PAIRS:
        c_u = along(i, u)
        s = scale1 if i < 7 else scale2
        even = s * (base + 4.5 * c_u * c_u)
        odd = s * (3.0 * c_u)
        out[i] = jnp.where(wall, p[i + 1], keep * p[i] + (even + odd))
        out[i + 1] = jnp.where(wall, p[i], keep * p[i + 1] + (even - odd))
    return out


def adjoint_parts(m, plain, factor):
    u = [factor * v for v in plain]
    even, odd = pairs_of(m)
    total = W0 * m[0] + W1 * (even[1] + even[3] + even[5])
    e79, e1113, e1517 = even[7] + even[9], even[11] + even[13], even[15] + even[17]
    total = total + W2 * (e79 + e1113 + e1517)
    first = [
        W1 * odd[1] + W2 * ((odd[7] + odd[9]) + (odd[11] + odd[13])),
        W1 * odd[3] + W2 * ((odd[7] - odd[9]) + (odd[15] + odd[17])),
        W1 * odd[5] + W2 * ((odd[11] - odd[13]) + (odd[15] - odd[17])),
    ]
    xx = W1 * even[1] + W2 * (e79 + e1113)
    yy = W1 * even[3] + W2 * (e79 + e1517)
    zz = W1 * even[5] + W2 * (e1113 + e1517)
    xy = W2 * (even[7] - even[9])
    xz = W2 * (even[11] - even[13])
    yz = W2 * (even[15] - even[17])
    second = [
        xx * u[0] + xy * u[1] + xz * u[2],
        xy * u[0] + yy * u[1] + yz * u[2],
        xz * u[0] + yz * u[1] + zz * u[2],
    ]

    def dot(p, q):
        return p[0] * q[0] + p[1] * q[1] + p[2] * q[2]

    scalar = total * (1.0 - 1.5 * dot(u, u)) + 3.0 * dot(u, first) + 4.5 * dot(u, second)
    vector = [3.0 * first[a] + 9.0 * second[a] - 3.0 * (u[a] * total) for a in range(3)]
    return scalar - dot(vector, u), vector


def adjoint_back(m, rest, vector, kind, factor):
    omega = rates(kind)
    keep = 1.0 - omega
    wall = kind == 2
    rest = omega * rest
    scale = omega * factor
    turned = [scale * v for v in vector]
    out = [None] * 19
    out[0] = jnp.where(wall, m[0], keep * m[0] + rest)
    for i in PAIRS:
        c_v = along(i, turned)
        out[i] = jnp.where(wall, m[i + 1], keep * m[i] + (rest + c_v))
        out[i + 1] = jnp.where(wall, m[i], keep * m[i + 1] + (rest - c_v))
    return out


def gradient(vector, density, plain, kind):
    inner = vector[0] * plain[0] + vector[1] * plain[1] + vector[2] * plain[2]
    return jnp.where(kind == 2, 0.0, rates(kind) * density * inner)


def kernel(
    sizes,
    forward_hbm,
    later_hbm,
    design_hbm,
    kind_hbm,
    region_hbm,
    adjoint_hbm,
    sensitivity_hbm,
    objective_ref,
    volumes_ref,
    forward,
    kind,
    region,
    pops,
    fields,
    macro,
    factors,
    grads,
    result,
    smooth,
    x_send,
    x_recv,
    y_send,
    y_recv,
    c_send,
    c_recv,
    stat_y,
    stat_x,
    load_sem,
    send_sem,
    recv_sem,
    sum_send,
    sum_recv,
):
    count_x, count_y = sizes
    nx, ny = kind.shape[0], kind.shape[1]
    me_x, me_y = lax.axis_index("gx"), lax.axis_index("gy")
    halves = range(0, ny, ROWS)

    def device(dx, dy):
        return (
            lax.rem(me_x + dx + count_x, count_x),
            lax.rem(me_y + dy + count_y, count_y),
        )

    inner = (pl.ds(1, nx), pl.ds(ROWS, ny))
    loads = [
        pltpu.make_async_copy(
            design_hbm, fields.at[0, pl.ds(RAD, nx), pl.ds(ROWS, ny)], load_sem.at[0]
        ),
        pltpu.make_async_copy(later_hbm, pops.at[LATER, :, inner[0], inner[1]], load_sem.at[1]),
        pltpu.make_async_copy(forward_hbm, forward, load_sem.at[2]),
        pltpu.make_async_copy(kind_hbm, kind, load_sem.at[3]),
        pltpu.make_async_copy(region_hbm, region, load_sem.at[4]),
    ]
    for load in loads:
        load.start()

    partners = {((dx + count_x) % count_x, (dy + count_y) % count_y) for dx, dy in DIRS}
    partners |= {(0, k) for k in range(1, count_y)} | {(k, 0) for k in range(1, count_x)}
    barrier = pltpu.get_barrier_semaphore()
    for dx, dy in sorted(partners):
        pl.semaphore_signal(barrier, inc=1, device_id=device(dx, dy), device_id_type=MESH)
    loads[0].wait()
    pl.semaphore_wait(barrier, len(partners))

    def field_copies(slot, exchange):
        copies = []
        for j, (dx, dy) in enumerate(DIRS):
            width = nx if dx == 0 else RAD
            source_x = {0: RAD, 1: nx, -1: RAD}[dx]
            target_x = {0: RAD, 1: 0, -1: nx + RAD}[dx]
            height = ny if dy == 0 else ROWS
            source_y = {0: ROWS, 1: ny, -1: ROWS}[dy]
            target_y = {0: ROWS, 1: 0, -1: ny + ROWS}[dy]
            copies.append(
                pltpu.make_async_remote_copy(
                    src_ref=fields.at[slot, pl.ds(source_x, width), pl.ds(source_y, height)],
                    dst_ref=fields.at[slot, pl.ds(target_x, width), pl.ds(target_y, height)],
                    send_sem=send_sem.at[exchange, j],
                    recv_sem=recv_sem.at[exchange, j],
                    device_id=device(dx, dy),
                    device_id_type=MESH,
                )
            )
        return copies

    def pops_copies(slot):
        copies = []
        for j, direction in enumerate(DIRS):
            if direction[1] == 0:
                source, target, k = x_send, x_recv, j
            elif direction[0] == 0:
                source, target, k = y_send, y_recv, j - 2
            else:
                source, target, k = c_send, c_recv, j - 4
            copies.append(
                pltpu.make_async_remote_copy(
                    src_ref=source.at[slot, k],
                    dst_ref=target.at[slot, k],
                    send_sem=send_sem.at[slot, j],
                    recv_sem=recv_sem.at[slot, j],
                    device_id=device(*direction),
                    device_id_type=MESH,
                )
            )
        return copies

    def send_pops(slot, sign):
        copies = pops_copies(slot)
        for j, (dx, dy) in enumerate(DIRS):
            x = nx if dx == 1 else 1
            y = ROWS + ny - 1 if dy == 1 else ROWS
            for k, i in enumerate(crossing((dx, dy), sign)):
                if dy == 0:
                    x_send[slot, j, k] = pops[slot, i, x, ROWS : ROWS + ny, :]
                elif dx == 0:
                    for row in range(nx):
                        y_send[slot, j - 2, k, row : row + 1, :] = pops[
                            slot, i, row + 1, y : y + 1, :
                        ]
                else:
                    c_send[slot, j - 4] = pops[slot, i, x, y : y + 1, :]
            copies[j].start()
        return copies

    def take_pops(slot, sign, copies):
        for j, (dx, dy) in enumerate(DIRS):
            copies[j].wait_recv()
            x = 0 if dx == 1 else nx + 1
            y = ROWS - 1 if dy == 1 else ROWS + ny
            for k, i in enumerate(crossing((dx, dy), sign)):
                if dy == 0:
                    pops[slot, i, x, ROWS : ROWS + ny, :] = x_recv[slot, j, k]
                elif dx == 0:
                    for row in range(nx):
                        pops[slot, i, row + 1, y : y + 1, :] = y_recv[
                            slot, j - 2, k, row : row + 1, :
                        ]
                else:
                    pops[slot, i, x, y : y + 1, :] = c_recv[slot, j - 4]

    def pick(slot, i, x, y, sign):
        cx, cy, cz = (sign * c for c in VELOCITY[i])
        value = pops[slot, i, x + 1 + cx, ROWS + y + cy : 2 * ROWS + y + cy, :]
        return shifted(value, cz)

    design_copies = field_copies(0, DESIGN)
    for copy in design_copies:
        copy.start()
    loads[1].wait()
    later_copies = send_pops(LATER, -1)
    for load in loads[2:]:
        load.wait()

    def macroscopic(x, carry):
        for y in halves:
            density, momenta = moments([forward[i, x, y : y + ROWS, :] for i in range(19)])
            inverse = 1.0 / density
            macro[0, x, y : y + ROWS, :] = density
            for a in range(3):
                macro[a + 1, x, y : y + ROWS, :] = momenta[a] * inverse
        return carry

    lax.fori_loop(0, nx, macroscopic, 0)
    inv_norm = inverse_norm((ROWS, kind.shape[2]))
    for copy in design_copies:
        copy.wait_recv()

    def first_step(x, sums):
        sums = list(sums)
        for y in halves:
            rows = slice(y, y + ROWS)
            kinds = kind[x, rows, :]
            design_cell = kinds == 1
            filtered = filter_taps(fields.at[0], x, y) * inv_norm
            factor = jnp.where(design_cell, 1.0 - BRINKMAN * (1.0 - filtered), 1.0)
            factors[x, rows, :] = factor
            regions = region[x, rows, :]
            inside = jnp.where(design_cell, filtered, 0.0)
            for r in range(REG):
                sums[r] = sums[r] + jnp.where(regions == r, inside, 0.0)
            post = collide(
                [forward[i, x, rows, :] for i in range(19)],
                macro[0, x, rows, :],
                [macro[a + 1, x, rows, :] for a in range(3)],
                kinds,
                factor,
            )
            for i in range(19):
                pops[POST, i, x + 1, ROWS + y : 2 * ROWS + y, :] = post[i]
        return tuple(sums)

    zero = jnp.zeros((ROWS, kind.shape[2]), jnp.float32)
    volumes = lax.fori_loop(0, nx, first_step, (zero,) * REG)
    post_copies = send_pops(POST, 1)
    take_pops(LATER, -1, later_copies)
    take_pops(POST, 1, post_copies)

    def middle_step(x, total):
        for y in halves:
            rows = slice(y, y + ROWS)
            kinds = kind[x, rows, :]
            factor = factors[x, rows, :]
            density, momenta = moments([pick(POST, i, x, y, -1) for i in range(19)])
            outlet = kinds == 4
            total = total + jnp.where(outlet, momenta[0], 0.0)
            inverse = 1.0 / density
            plain = [m * inverse for m in momenta]
            incoming = [pick(LATER, i, x, y, 1) for i in range(19)]
            rest, vector = adjoint_parts(incoming, plain, factor)
            grads[x, rows, :] = gradient(vector, density, plain, kinds)
            middle = adjoint_back(incoming, rest, vector, kinds, factor)
            source = jnp.where(outlet, 1.0, 0.0)
            for i in range(19):
                value = middle[i]
                if VELOCITY[i][0] == 1:
                    value = value + source
                elif VELOCITY[i][0] == -1:
                    value = value - source
                pops[MIDDLE, i, x + 1, ROWS + y : 2 * ROWS + y, :] = value
        return total

    objective = lax.fori_loop(0, nx, middle_step, zero)
    middle_copies = send_pops(MIDDLE, -1)

    def spread(stat, count, me, sem, place):
        copies = []
        for k in range(1, count):
            copies.append(
                pltpu.make_async_remote_copy(
                    src_ref=stat.at[me],
                    dst_ref=stat.at[me],
                    send_sem=sum_send.at[sem, k],
                    recv_sem=sum_recv.at[sem, k],
                    device_id=place(k),
                    device_id_type=MESH,
                )
            )
        for copy in copies:
            copy.start()
        return copies

    for r in range(REG):
        stat_y[me_y, r : r + 1, :] = jnp.sum(volumes[r], axis=0, keepdims=True)
    stat_y[me_y, REG : REG + 1, :] = jnp.sum(objective, axis=0, keepdims=True)
    stat_y[me_y, REG + 1 :, :] = jnp.zeros((REG - 1, zero.shape[1]), jnp.float32)
    sums_y = spread(stat_y, count_y, me_y, 0, lambda k: device(0, k))
    take_pops(MIDDLE, -1, middle_copies)

    def second_step(x, carry):
        for y in halves:
            rows = slice(y, y + ROWS)
            kinds = kind[x, rows, :]
            factor = factors[x, rows, :]
            density = macro[0, x, rows, :]
            plain = [macro[a + 1, x, rows, :] for a in range(3)]
            incoming = [pick(MIDDLE, i, x, y, 1) for i in range(19)]
            rest, vector = adjoint_parts(incoming, plain, factor)
            grad = grads[x, rows, :] + gradient(vector, density, plain, kinds)
            raw = jnp.where(kinds == 1, BRINKMAN * grad, 0.0) * inv_norm
            fields[1, x + RAD, ROWS + y : 2 * ROWS + y, :] = raw
            back = adjoint_back(incoming, rest, vector, kinds, factor)
            for i in range(19):
                result[i, x, rows, :] = back[i]
        return carry

    lax.fori_loop(0, nx, second_step, 0)
    raw_copies = field_copies(1, RAW)
    for copy in raw_copies:
        copy.start()
    store = pltpu.make_async_copy(result, adjoint_hbm, load_sem.at[5])
    store.start()

    for copy in sums_y:
        copy.wait()
    subtotal = stat_y[0]
    for k in range(1, count_y):
        subtotal = subtotal + stat_y[k]
    stat_x[me_x] = subtotal
    sums_x = spread(stat_x, count_x, me_x, 1, lambda k: device(k, 0))
    for copy in raw_copies:
        copy.wait_recv()

    def last_step(x, carry):
        for y in halves:
            smooth[x, y : y + ROWS, :] = filter_taps(fields.at[1], x, y)
        return carry

    lax.fori_loop(0, nx, last_step, 0)
    store_smooth = pltpu.make_async_copy(smooth, sensitivity_hbm, load_sem.at[6])
    store_smooth.start()
    for copy in sums_x:
        copy.wait()
    total = stat_x[0]
    for k in range(1, count_x):
        total = total + stat_x[k]
    total = jnp.sum(total, axis=1, keepdims=True)
    for r in range(REG):
        volumes_ref[r] = total[r, 0]
    objective_ref[0] = total[REG, 0]
    for copies in (design_copies, later_copies, post_copies, middle_copies, raw_copies):
        for copy in copies:
            copy.wait_send()
    store.wait()
    store_smooth.wait()


def per_device(sizes, forward_pops, later_adjoint, design, node_type, region):
    nx, ny, nz = design.shape
    f32 = jnp.float32
    anywhere = pl.BlockSpec(memory_space=pl.ANY)
    scalars = pl.BlockSpec(memory_space=pltpu.SMEM)
    block = (nx, ny, nz)
    most = max(sizes)
    adjoint, sensitivity, objective, volumes = pl.pallas_call(
        functools.partial(kernel, sizes),
        out_shape=(
            jax.ShapeDtypeStruct((19,) + block, f32),
            jax.ShapeDtypeStruct(block, f32),
            jax.ShapeDtypeStruct((1,), f32),
            jax.ShapeDtypeStruct((REG,), f32),
        ),
        in_specs=[anywhere] * 5,
        out_specs=(anywhere, anywhere, scalars, scalars),
        scratch_shapes=[
            pltpu.VMEM((19,) + block, f32),
            pltpu.VMEM(block, jnp.int32),
            pltpu.VMEM(block, jnp.int32),
            pltpu.VMEM((3, 19, nx + 2, ny + 2 * ROWS, nz), f32),
            pltpu.VMEM((2, nx + 2 * RAD, ny + 2 * ROWS, nz), f32),
            pltpu.VMEM((4,) + block, f32),
            pltpu.VMEM(block, f32),
            pltpu.VMEM(block, f32),
            pltpu.VMEM((19,) + block, f32),
            pltpu.VMEM(block, f32),
            pltpu.VMEM((3, 2, 5, ny, nz), f32),
            pltpu.VMEM((3, 2, 5, ny, nz), f32),
            pltpu.VMEM((3, 2, 5, nx, nz), f32),
            pltpu.VMEM((3, 2, 5, nx, nz), f32),
            pltpu.VMEM((3, 4, 1, nz), f32),
            pltpu.VMEM((3, 4, 1, nz), f32),
            pltpu.VMEM((sizes[1], 2 * REG, nz), f32),
            pltpu.VMEM((sizes[0], 2 * REG, nz), f32),
            pltpu.SemaphoreType.DMA((7,)),
            pltpu.SemaphoreType.DMA((5, 8)),
            pltpu.SemaphoreType.DMA((5, 8)),
            pltpu.SemaphoreType.DMA((2, most)),
            pltpu.SemaphoreType.DMA((2, most)),
        ],
        compiler_params=pltpu.CompilerParams(
            collective_id=0, has_side_effects=True, vmem_limit_bytes=40 * 1024 * 1024
        ),
        name="lattice_adjoint",
    )(forward_pops, later_adjoint, design, node_type, region)
    return adjoint, sensitivity, objective.reshape(()), volumes


def solution(mesh):
    sizes = (mesh.shape["gx"], mesh.shape["gy"])
    in_specs = (
        P(None, "gx", "gy", None),
        P(None, "gx", "gy", None),
        P("gx", "gy", None),
        P("gx", "gy", None),
        P("gx", "gy", None),
    )
    out_specs = (P(None, "gx", "gy", None), P("gx", "gy", None), P(), P())
    return jax.shard_map(
        functools.partial(per_device, sizes),
        mesh=mesh,
        in_specs=in_specs,
        out_specs=out_specs,
        check_vma=False,
    )
```

```python
import functools
import math

import jax
import jax.numpy as jnp
from jax import lax
from jax.experimental import pallas as pl
from jax.experimental.pallas import tpu as pltpu
from jax.sharding import PartitionSpec as P

RAD = 3
REG = 8
MESH = pl.DeviceIdType.MESH

VELOCITY = [
    (0, 0, 0),
    (1, 0, 0),
    (-1, 0, 0),
    (0, 1, 0),
    (0, -1, 0),
    (0, 0, 1),
    (0, 0, -1),
    (1, 1, 0),
    (-1, -1, 0),
    (1, -1, 0),
    (-1, 1, 0),
    (1, 0, 1),
    (-1, 0, -1),
    (1, 0, -1),
    (-1, 0, 1),
    (0, 1, 1),
    (0, -1, -1),
    (0, 1, -1),
    (0, -1, 1),
]
W0, W1, W2 = 1.0 / 3.0, 1.0 / 18.0, 1.0 / 36.0
PAIRS = [1, 3, 5, 7, 9, 11, 13, 15, 17]
OPPOSITE = [0, 2, 1, 4, 3, 6, 5, 8, 7, 10, 9, 12, 11, 14, 13, 16, 15, 18, 17]
RELAXATION = 1.0 / 0.6
BRINKMAN = 0.9

DIRS = [(1, 0), (-1, 0), (0, 1), (0, -1), (1, 1), (-1, -1), (1, -1), (-1, 1)]
ROWS = 8
POST, LATER, MIDDLE = 0, 1, 2
DESIGN, RAW = 3, 4


def weight(a, b, c):
    return max(RAD + 1 - math.sqrt(a * a + b * b + c * c), 0.0)


def crossing(direction, sign):
    return [
        i
        for i in range(19)
        if all(
            direction[a] == 0 or sign * VELOCITY[i][a] == direction[a] for a in range(2)
        )
    ]


def lanes(shape):
    return lax.broadcasted_iota(jnp.int32, shape, len(shape) - 1)


def shifted(value, offset):
    if offset == 0:
        return value
    depth = value.shape[-1]
    z = lanes(value.shape)
    rolled = pltpu.roll(value, (-offset) % depth, value.ndim - 1)
    inside = z < depth - offset if offset > 0 else z >= -offset
    return jnp.where(inside, rolled, 0.0)


def inverse_norm(shape):
    depth = shape[-1]
    z = lanes(shape)
    span = range(-RAD, RAD + 1)
    norm = jnp.zeros(shape, jnp.float32)
    for c in span:
        layer = sum(weight(a, b, c) for a in span for b in span)
        inside = (z + c >= 0) & (z + c < depth)
        norm = norm + jnp.where(inside, layer, 0.0)
    return 1.0 / norm


def filter_taps(field, x, y):
    classes = {}
    for a in range(-RAD, RAD + 1):
        for b in range(-RAD, RAD + 1):
            if weight(a, b, 0) > 0:
                value = field[x + RAD + a, ROWS + y + b : 2 * ROWS + y + b, :]
                key = a * a + b * b
                classes[key] = classes[key] + value if key in classes else value
    result = None
    for c in range(RAD + 1):
        layer = None
        for key, value in classes.items():
            w = max(RAD + 1 - math.sqrt(key + c * c), 0.0)
            if w > 0:
                layer = w * value if layer is None else layer + w * value
        if c == 0:
            result = layer
        else:
            result = result + shifted(layer, c) + shifted(layer, -c)
    return result


def pairs_of(p):
    return (
        {i: p[i] + p[i + 1] for i in PAIRS},
        {i: p[i] - p[i + 1] for i in PAIRS},
    )


def moments(p):
    even, odd = pairs_of(p)
    density = p[0] + (
        ((even[1] + even[3]) + (even[5] + even[7]))
        + ((even[9] + even[11]) + (even[13] + (even[15] + even[17])))
    )
    momenta = [
        (odd[1] + odd[7]) + (odd[9] + (odd[11] + odd[13])),
        (odd[3] + odd[7]) + (odd[15] + odd[17] - odd[9]),
        (odd[5] + odd[11]) + (odd[15] - odd[13] - odd[17]),
    ]
    return density, momenta


def along(i, u):
    total = None
    for a in range(3):
        if VELOCITY[i][a] != 0:
            if total is None:
                total = u[a]
            elif VELOCITY[i][a] > 0:
                total = total + u[a]
            else:
                total = total - u[a]
    return total


def rates(kind):
    return jnp.where(kind <= 1, RELAXATION, 1.0)


def collide(p, density, plain, kind, factor):
    u = [factor * v for v in plain]
    base = 1.0 - 1.5 * (u[0] * u[0] + u[1] * u[1] + u[2] * u[2])
    omega = rates(kind)
    keep = 1.0 - omega
    wall = kind == 2
    scale = omega * density
    scale1 = W1 * scale
    scale2 = W2 * scale
    out = [None] * 19
    out[0] = jnp.where(wall, p[0], keep * p[0] + (W0 * scale) * base)
    for i in PAIRS:
        c_u = along(i, u)
        s = scale1 if i < 7 else scale2
        even = s * (base + 4.5 * c_u * c_u)
        odd = s * (3.0 * c_u)
        out[i] = jnp.where(wall, p[i + 1], keep * p[i] + (even + odd))
        out[i + 1] = jnp.where(wall, p[i], keep * p[i + 1] + (even - odd))
    return out


def adjoint_parts(m, plain, factor):
    u = [factor * v for v in plain]
    even, odd = pairs_of(m)
    total = W0 * m[0] + W1 * (even[1] + even[3] + even[5])
    e79, e1113, e1517 = even[7] + even[9], even[11] + even[13], even[15] + even[17]
    total = total + W2 * (e79 + e1113 + e1517)
    first = [
        W1 * odd[1] + W2 * ((odd[7] + odd[9]) + (odd[11] + odd[13])),
        W1 * odd[3] + W2 * ((odd[7] - odd[9]) + (odd[15] + odd[17])),
        W1 * odd[5] + W2 * ((odd[11] - odd[13]) + (odd[15] - odd[17])),
    ]
    xx = W1 * even[1] + W2 * (e79 + e1113)
    yy = W1 * even[3] + W2 * (e79 + e1517)
    zz = W1 * even[5] + W2 * (e1113 + e1517)
    xy = W2 * (even[7] - even[9])
    xz = W2 * (even[11] - even[13])
    yz = W2 * (even[15] - even[17])
    second = [
        xx * u[0] + xy * u[1] + xz * u[2],
        xy * u[0] + yy * u[1] + yz * u[2],
        xz * u[0] + yz * u[1] + zz * u[2],
    ]

    def dot(p, q):
        return p[0] * q[0] + p[1] * q[1] + p[2] * q[2]

    scalar = total * (1.0 - 1.5 * dot(u, u)) + 3.0 * dot(u, first) + 4.5 * dot(u, second)
    vector = [3.0 * first[a] + 9.0 * second[a] - 3.0 * (u[a] * total) for a in range(3)]
    return scalar - dot(vector, u), vector


def adjoint_back(m, rest, vector, kind, factor):
    omega = rates(kind)
    keep = 1.0 - omega
    wall = kind == 2
    rest = omega * rest
    scale = omega * factor
    turned = [scale * v for v in vector]
    out = [None] * 19
    out[0] = jnp.where(wall, m[0], keep * m[0] + rest)
    for i in PAIRS:
        c_v = along(i, turned)
        out[i] = jnp.where(wall, m[i + 1], keep * m[i] + (rest + c_v))
        out[i + 1] = jnp.where(wall, m[i], keep * m[i + 1] + (rest - c_v))
    return out


def gradient(vector, density, plain, kind):
    inner = vector[0] * plain[0] + vector[1] * plain[1] + vector[2] * plain[2]
    return jnp.where(kind == 2, 0.0, rates(kind) * density * inner)


def kernel(
    sizes,
    forward_hbm,
    later_hbm,
    design_hbm,
    kind_hbm,
    region_hbm,
    adjoint_hbm,
    sensitivity_hbm,
    objective_ref,
    volumes_ref,
    forward,
    kind,
    region,
    pops,
    fields,
    macro,
    factors,
    grads,
    result,
    smooth,
    x_send,
    x_recv,
    y_send,
    y_recv,
    c_send,
    c_recv,
    stat_y,
    stat_x,
    load_sem,
    send_sem,
    recv_sem,
    sum_send,
    sum_recv,
):
    count_x, count_y = sizes
    nx, ny = kind.shape[0], kind.shape[1]
    me_x, me_y = lax.axis_index("gx"), lax.axis_index("gy")
    halves = range(0, ny, ROWS)

    def device(dx, dy):
        return (
            lax.rem(me_x + dx + count_x, count_x),
            lax.rem(me_y + dy + count_y, count_y),
        )

    inner = (pl.ds(1, nx), pl.ds(ROWS, ny))
    loads = [
        pltpu.make_async_copy(
            design_hbm, fields.at[0, pl.ds(RAD, nx), pl.ds(ROWS, ny)], load_sem.at[0]
        ),
        pltpu.make_async_copy(later_hbm, pops.at[LATER, :, inner[0], inner[1]], load_sem.at[1]),
        pltpu.make_async_copy(forward_hbm, forward, load_sem.at[2]),
        pltpu.make_async_copy(kind_hbm, kind, load_sem.at[3]),
        pltpu.make_async_copy(region_hbm, region, load_sem.at[4]),
    ]
    for load in loads:
        load.start()

    partners = {((dx + count_x) % count_x, (dy + count_y) % count_y) for dx, dy in DIRS}
    partners |= {(0, k) for k in range(1, count_y)} | {(k, 0) for k in range(1, count_x)}
    barrier = pltpu.get_barrier_semaphore()
    for dx, dy in sorted(partners):
        pl.semaphore_signal(barrier, inc=1, device_id=device(dx, dy), device_id_type=MESH)
    loads[0].wait()
    pl.semaphore_wait(barrier, len(partners))

    def field_copies(slot, exchange):
        copies = []
        for j, (dx, dy) in enumerate(DIRS):
            width = nx if dx == 0 else RAD
            source_x = {0: RAD, 1: nx, -1: RAD}[dx]
            target_x = {0: RAD, 1: 0, -1: nx + RAD}[dx]
            height = ny if dy == 0 else ROWS
            source_y = {0: ROWS, 1: ny, -1: ROWS}[dy]
            target_y = {0: ROWS, 1: 0, -1: ny + ROWS}[dy]
            copies.append(
                pltpu.make_async_remote_copy(
                    src_ref=fields.at[slot, pl.ds(source_x, width), pl.ds(source_y, height)],
                    dst_ref=fields.at[slot, pl.ds(target_x, width), pl.ds(target_y, height)],
                    send_sem=send_sem.at[exchange, j],
                    recv_sem=recv_sem.at[exchange, j],
                    device_id=device(dx, dy),
                    device_id_type=MESH,
                )
            )
        return copies

    def pops_copies(slot):
        copies = []
        for j, direction in enumerate(DIRS):
            if direction[1] == 0:
                source, target, k = x_send, x_recv, j
            elif direction[0] == 0:
                source, target, k = y_send, y_recv, j - 2
            else:
                source, target, k = c_send, c_recv, j - 4
            copies.append(
                pltpu.make_async_remote_copy(
                    src_ref=source.at[slot, k],
                    dst_ref=target.at[slot, k],
                    send_sem=send_sem.at[slot, j],
                    recv_sem=recv_sem.at[slot, j],
                    device_id=device(*direction),
                    device_id_type=MESH,
                )
            )
        return copies

    def send_pops(slot, sign):
        copies = pops_copies(slot)
        for j, (dx, dy) in enumerate(DIRS):
            x = nx if dx == 1 else 1
            y = ROWS + ny - 1 if dy == 1 else ROWS
            for k, i in enumerate(crossing((dx, dy), sign)):
                if dy == 0:
                    x_send[slot, j, k] = pops[slot, i, x, ROWS : ROWS + ny, :]
                elif dx == 0:
                    for row in range(nx):
                        y_send[slot, j - 2, k, row : row + 1, :] = pops[
                            slot, i, row + 1, y : y + 1, :
                        ]
                else:
                    c_send[slot, j - 4] = pops[slot, i, x, y : y + 1, :]
            copies[j].start()
        return copies

    def take_pops(slot, sign, copies):
        for j, (dx, dy) in enumerate(DIRS):
            copies[j].wait_recv()
            x = 0 if dx == 1 else nx + 1
            y = ROWS - 1 if dy == 1 else ROWS + ny
            for k, i in enumerate(crossing((dx, dy), sign)):
                if dy == 0:
                    pops[slot, i, x, ROWS : ROWS + ny, :] = x_recv[slot, j, k]
                elif dx == 0:
                    for row in range(nx):
                        pops[slot, i, row + 1, y : y + 1, :] = y_recv[
                            slot, j - 2, k, row : row + 1, :
                        ]
                else:
                    pops[slot, i, x, y : y + 1, :] = c_recv[slot, j - 4]

    def pick(slot, i, x, y, sign):
        cx, cy, cz = (sign * c for c in VELOCITY[i])
        value = pops[slot, i, x + 1 + cx, ROWS + y + cy : 2 * ROWS + y + cy, :]
        return shifted(value, cz)

    design_copies = field_copies(0, DESIGN)
    for copy in design_copies:
        copy.start()
    loads[1].wait()
    later_copies = send_pops(LATER, -1)
    for load in loads[2:]:
        load.wait()

    def macroscopic(x, carry):
        for y in halves:
            density, momenta = moments([forward[i, x, y : y + ROWS, :] for i in range(19)])
            inverse = 1.0 / density
            macro[0, x, y : y + ROWS, :] = density
            for a in range(3):
                macro[a + 1, x, y : y + ROWS, :] = momenta[a] * inverse
        return carry

    lax.fori_loop(0, nx, macroscopic, 0)
    inv_norm = inverse_norm((ROWS, kind.shape[2]))
    for copy in design_copies:
        copy.wait_recv()

    def first_step(x, sums):
        sums = list(sums)
        for y in halves:
            rows = slice(y, y + ROWS)
            kinds = kind[x, rows, :]
            design_cell = kinds == 1
            filtered = filter_taps(fields.at[0], x, y) * inv_norm
            factor = jnp.where(design_cell, 1.0 - BRINKMAN * (1.0 - filtered), 1.0)
            factors[x, rows, :] = factor
            regions = region[x, rows, :]
            inside = jnp.where(design_cell, filtered, 0.0)
            for r in range(REG):
                sums[r] = sums[r] + jnp.where(regions == r, inside, 0.0)
            post = collide(
                [forward[i, x, rows, :] for i in range(19)],
                macro[0, x, rows, :],
                [macro[a + 1, x, rows, :] for a in range(3)],
                kinds,
                factor,
            )
            for i in range(19):
                pops[POST, i, x + 1, ROWS + y : 2 * ROWS + y, :] = post[i]
        return tuple(sums)

    zero = jnp.zeros((ROWS, kind.shape[2]), jnp.float32)
    volumes = lax.fori_loop(0, nx, first_step, (zero,) * REG)
    post_copies = send_pops(POST, 1)
    take_pops(LATER, -1, later_copies)
    take_pops(POST, 1, post_copies)

    def middle_step(x, total):
        for y in halves:
            rows = slice(y, y + ROWS)
            kinds = kind[x, rows, :]
            factor = factors[x, rows, :]
            density, momenta = moments([pick(POST, i, x, y, -1) for i in range(19)])
            outlet = kinds == 4
            total = total + jnp.where(outlet, momenta[0], 0.0)
            inverse = 1.0 / density
            plain = [m * inverse for m in momenta]
            incoming = [pick(LATER, i, x, y, 1) for i in range(19)]
            rest, vector = adjoint_parts(incoming, plain, factor)
            grads[x, rows, :] = gradient(vector, density, plain, kinds)
            middle = adjoint_back(incoming, rest, vector, kinds, factor)
            source = jnp.where(outlet, 1.0, 0.0)
            for i in range(19):
                value = middle[i]
                if VELOCITY[i][0] == 1:
                    value = value + source
                elif VELOCITY[i][0] == -1:
                    value = value - source
                pops[MIDDLE, i, x + 1, ROWS + y : 2 * ROWS + y, :] = value
        return total

    objective = lax.fori_loop(0, nx, middle_step, zero)
    middle_copies = send_pops(MIDDLE, -1)

    def spread(stat, count, me, sem, place):
        copies = []
        for k in range(1, count):
            copies.append(
                pltpu.make_async_remote_copy(
                    src_ref=stat.at[me],
                    dst_ref=stat.at[me],
                    send_sem=sum_send.at[sem, k],
                    recv_sem=sum_recv.at[sem, k],
                    device_id=place(k),
                    device_id_type=MESH,
                )
            )
        for copy in copies:
            copy.start()
        return copies

    for r in range(REG):
        stat_y[me_y, r : r + 1, :] = jnp.sum(volumes[r], axis=0, keepdims=True)
    stat_y[me_y, REG : REG + 1, :] = jnp.sum(objective, axis=0, keepdims=True)
    stat_y[me_y, REG + 1 :, :] = jnp.zeros((REG - 1, zero.shape[1]), jnp.float32)
    sums_y = spread(stat_y, count_y, me_y, 0, lambda k: device(0, k))
    take_pops(MIDDLE, -1, middle_copies)

    def second_step(x, carry):
        for y in halves:
            rows = slice(y, y + ROWS)
            kinds = kind[x, rows, :]
            factor = factors[x, rows, :]
            density = macro[0, x, rows, :]
            plain = [macro[a + 1, x, rows, :] for a in range(3)]
            incoming = [pick(MIDDLE, i, x, y, 1) for i in range(19)]
            rest, vector = adjoint_parts(incoming, plain, factor)
            grad = grads[x, rows, :] + gradient(vector, density, plain, kinds)
            raw = jnp.where(kinds == 1, BRINKMAN * grad, 0.0) * inv_norm
            fields[1, x + RAD, ROWS + y : 2 * ROWS + y, :] = raw
            back = adjoint_back(incoming, rest, vector, kinds, factor)
            for i in range(19):
                result[i, x, rows, :] = back[i]
        return carry

    lax.fori_loop(0, nx, second_step, 0)
    raw_copies = field_copies(1, RAW)
    for copy in raw_copies:
        copy.start()
    store = pltpu.make_async_copy(result, adjoint_hbm, load_sem.at[5])
    store.start()

    for copy in sums_y:
        copy.wait()
    subtotal = stat_y[0]
    for k in range(1, count_y):
        subtotal = subtotal + stat_y[k]
    stat_x[me_x] = subtotal
    sums_x = spread(stat_x, count_x, me_x, 1, lambda k: device(k, 0))
    for copy in raw_copies:
        copy.wait_recv()

    def last_step(x, carry):
        for y in halves:
            smooth[x, y : y + ROWS, :] = filter_taps(fields.at[1], x, y)
        return carry

    lax.fori_loop(0, nx, last_step, 0)
    store_smooth = pltpu.make_async_copy(smooth, sensitivity_hbm, load_sem.at[6])
    store_smooth.start()
    for copy in sums_x:
        copy.wait()
    total = stat_x[0]
    for k in range(1, count_x):
        total = total + stat_x[k]
    total = jnp.sum(total, axis=1, keepdims=True)
    for r in range(REG):
        volumes_ref[r] = total[r, 0]
    objective_ref[0] = total[REG, 0]
    for copies in (design_copies, later_copies, post_copies, middle_copies, raw_copies):
        for copy in copies:
            copy.wait_send()
    store.wait()
    store_smooth.wait()


def per_device(sizes, forward_pops, later_adjoint, design, node_type, region):
    nx, ny, nz = design.shape
    f32 = jnp.float32
    anywhere = pl.BlockSpec(memory_space=pl.ANY)
    scalars = pl.BlockSpec(memory_space=pltpu.SMEM)
    block = (nx, ny, nz)
    most = max(sizes)
    adjoint, sensitivity, objective, volumes = pl.pallas_call(
        functools.partial(kernel, sizes),
        out_shape=(
            jax.ShapeDtypeStruct((19,) + block, f32),
            jax.ShapeDtypeStruct(block, f32),
            jax.ShapeDtypeStruct((1,), f32),
            jax.ShapeDtypeStruct((REG,), f32),
        ),
        in_specs=[anywhere] * 5,
        out_specs=(anywhere, anywhere, scalars, scalars),
        scratch_shapes=[
            pltpu.VMEM((19,) + block, f32),
            pltpu.VMEM(block, jnp.int32),
            pltpu.VMEM(block, jnp.int32),
            pltpu.VMEM((3, 19, nx + 2, ny + 2 * ROWS, nz), f32),
            pltpu.VMEM((2, nx + 2 * RAD, ny + 2 * ROWS, nz), f32),
            pltpu.VMEM((4,) + block, f32),
            pltpu.VMEM(block, f32),
            pltpu.VMEM(block, f32),
            pltpu.VMEM((19,) + block, f32),
            pltpu.VMEM(block, f32),
            pltpu.VMEM((3, 2, 5, ny, nz), f32),
            pltpu.VMEM((3, 2, 5, ny, nz), f32),
            pltpu.VMEM((3, 2, 5, nx, nz), f32),
            pltpu.VMEM((3, 2, 5, nx, nz), f32),
            pltpu.VMEM((3, 4, 1, nz), f32),
            pltpu.VMEM((3, 4, 1, nz), f32),
            pltpu.VMEM((sizes[1], 2 * REG, nz), f32),
            pltpu.VMEM((sizes[0], 2 * REG, nz), f32),
            pltpu.SemaphoreType.DMA((7,)),
            pltpu.SemaphoreType.DMA((5, 8)),
            pltpu.SemaphoreType.DMA((5, 8)),
            pltpu.SemaphoreType.DMA((2, most)),
            pltpu.SemaphoreType.DMA((2, most)),
        ],
        compiler_params=pltpu.CompilerParams(
            collective_id=0, has_side_effects=True, vmem_limit_bytes=60 * 1024 * 1024
        ),
        name="lattice_adjoint",
    )(forward_pops, later_adjoint, design, node_type, region)
    return adjoint, sensitivity, objective.reshape(()), volumes


def solution(mesh):
    sizes = (mesh.shape["gx"], mesh.shape["gy"])
    in_specs = (
        P(None, "gx", "gy", None),
        P(None, "gx", "gy", None),
        P("gx", "gy", None),
        P("gx", "gy", None),
        P("gx", "gy", None),
    )
    out_specs = (P(None, "gx", "gy", None), P("gx", "gy", None), P(), P())
    return jax.shard_map(
        functools.partial(per_device, sizes),
        mesh=mesh,
        in_specs=in_specs,
        out_specs=out_specs,
        check_vma=False,
    )
```

```python
import functools
import math

import jax
import jax.numpy as jnp
from jax import lax
from jax.experimental import pallas as pl
from jax.experimental.pallas import tpu as pltpu
from jax.sharding import PartitionSpec as P

RAD = 3
REG = 8
MESH = pl.DeviceIdType.MESH

VELOCITY = [
    (0, 0, 0),
    (1, 0, 0),
    (-1, 0, 0),
    (0, 1, 0),
    (0, -1, 0),
    (0, 0, 1),
    (0, 0, -1),
    (1, 1, 0),
    (-1, -1, 0),
    (1, -1, 0),
    (-1, 1, 0),
    (1, 0, 1),
    (-1, 0, -1),
    (1, 0, -1),
    (-1, 0, 1),
    (0, 1, 1),
    (0, -1, -1),
    (0, 1, -1),
    (0, -1, 1),
]
W0, W1, W2 = 1.0 / 3.0, 1.0 / 18.0, 1.0 / 36.0
PAIRS = [1, 3, 5, 7, 9, 11, 13, 15, 17]
OPPOSITE = [0, 2, 1, 4, 3, 6, 5, 8, 7, 10, 9, 12, 11, 14, 13, 16, 15, 18, 17]
RELAXATION = 1.0 / 0.6
BRINKMAN = 0.9

DIRS = [(1, 0), (-1, 0), (0, 1), (0, -1), (1, 1), (-1, -1), (1, -1), (-1, 1)]
ALONG_Y = [2, 3]
ACROSS_X = [0, 1, 4, 5, 6, 7]
ROWS = 8
POST, LATER, MIDDLE = 0, 1, 2
DESIGN, RAW = 3, 4


def weight(a, b, c):
    return max(RAD + 1 - math.sqrt(a * a + b * b + c * c), 0.0)


def crossing(direction, sign):
    return [
        i
        for i in range(19)
        if all(
            direction[a] == 0 or sign * VELOCITY[i][a] == direction[a] for a in range(2)
        )
    ]


def lanes(shape):
    return lax.broadcasted_iota(jnp.int32, shape, len(shape) - 1)


def shifted(value, offset):
    if offset == 0:
        return value
    depth = value.shape[-1]
    z = lanes(value.shape)
    rolled = pltpu.roll(value, (-offset) % depth, value.ndim - 1)
    inside = z < depth - offset if offset > 0 else z >= -offset
    return jnp.where(inside, rolled, 0.0)


def inverse_norm(shape):
    depth = shape[-1]
    z = lanes(shape)
    span = range(-RAD, RAD + 1)
    norm = jnp.zeros(shape, jnp.float32)
    for c in span:
        layer = sum(weight(a, b, c) for a in span for b in span)
        inside = (z + c >= 0) & (z + c < depth)
        norm = norm + jnp.where(inside, layer, 0.0)
    return 1.0 / norm


def filter_taps(field, x, y):
    classes = {}
    for a in range(-RAD, RAD + 1):
        for b in range(-RAD, RAD + 1):
            if weight(a, b, 0) > 0:
                value = field[x + RAD + a, ROWS + y + b : 2 * ROWS + y + b, :]
                key = a * a + b * b
                classes[key] = classes[key] + value if key in classes else value
    result = None
    for c in range(RAD + 1):
        layer = None
        for key, value in classes.items():
            w = max(RAD + 1 - math.sqrt(key + c * c), 0.0)
            if w > 0:
                layer = w * value if layer is None else layer + w * value
        if c == 0:
            result = layer
        else:
            result = result + shifted(layer, c) + shifted(layer, -c)
    return result


def pairs_of(p):
    return (
        {i: p[i] + p[i + 1] for i in PAIRS},
        {i: p[i] - p[i + 1] for i in PAIRS},
    )


def moments(p):
    even, odd = pairs_of(p)
    density = p[0] + (
        ((even[1] + even[3]) + (even[5] + even[7]))
        + ((even[9] + even[11]) + (even[13] + (even[15] + even[17])))
    )
    momenta = [
        (odd[1] + odd[7]) + (odd[9] + (odd[11] + odd[13])),
        (odd[3] + odd[7]) + (odd[15] + odd[17] - odd[9]),
        (odd[5] + odd[11]) + (odd[15] - odd[13] - odd[17]),
    ]
    return density, momenta


def along(i, u):
    total = None
    for a in range(3):
        if VELOCITY[i][a] != 0:
            if total is None:
                total = u[a]
            elif VELOCITY[i][a] > 0:
                total = total + u[a]
            else:
                total = total - u[a]
    return total


def rates(kind):
    return jnp.where(kind <= 1, RELAXATION, 1.0)


def collide(p, density, plain, kind, factor):
    u = [factor * v for v in plain]
    base = 1.0 - 1.5 * (u[0] * u[0] + u[1] * u[1] + u[2] * u[2])
    omega = rates(kind)
    keep = 1.0 - omega
    wall = kind == 2
    scale = omega * density
    scale1 = W1 * scale
    scale2 = W2 * scale
    out = [None] * 19
    out[0] = jnp.where(wall, p[0], keep * p[0] + (W0 * scale) * base)
    for i in PAIRS:
        c_u = along(i, u)
        s = scale1 if i < 7 else scale2
        even = s * (base + 4.5 * c_u * c_u)
        odd = s * (3.0 * c_u)
        out[i] = jnp.where(wall, p[i + 1], keep * p[i] + (even + odd))
        out[i + 1] = jnp.where(wall, p[i], keep * p[i + 1] + (even - odd))
    return out


def adjoint_parts(m, plain, factor):
    u = [factor * v for v in plain]
    even, odd = pairs_of(m)
    total = W0 * m[0] + W1 * (even[1] + even[3] + even[5])
    e79, e1113, e1517 = even[7] + even[9], even[11] + even[13], even[15] + even[17]
    total = total + W2 * (e79 + e1113 + e1517)
    first = [
        W1 * odd[1] + W2 * ((odd[7] + odd[9]) + (odd[11] + odd[13])),
        W1 * odd[3] + W2 * ((odd[7] - odd[9]) + (odd[15] + odd[17])),
        W1 * odd[5] + W2 * ((odd[11] - odd[13]) + (odd[15] - odd[17])),
    ]
    xx = W1 * even[1] + W2 * (e79 + e1113)
    yy = W1 * even[3] + W2 * (e79 + e1517)
    zz = W1 * even[5] + W2 * (e1113 + e1517)
    xy = W2 * (even[7] - even[9])
    xz = W2 * (even[11] - even[13])
    yz = W2 * (even[15] - even[17])
    second = [
        xx * u[0] + xy * u[1] + xz * u[2],
        xy * u[0] + yy * u[1] + yz * u[2],
        xz * u[0] + yz * u[1] + zz * u[2],
    ]

    def dot(p, q):
        return p[0] * q[0] + p[1] * q[1] + p[2] * q[2]

    scalar = total * (1.0 - 1.5 * dot(u, u)) + 3.0 * dot(u, first) + 4.5 * dot(u, second)
    vector = [3.0 * first[a] + 9.0 * second[a] - 3.0 * (u[a] * total) for a in range(3)]
    return scalar - dot(vector, u), vector


def adjoint_back(m, rest, vector, kind, factor):
    omega = rates(kind)
    keep = 1.0 - omega
    wall = kind == 2
    rest = omega * rest
    scale = omega * factor
    turned = [scale * v for v in vector]
    out = [None] * 19
    out[0] = jnp.where(wall, m[0], keep * m[0] + rest)
    for i in PAIRS:
        c_v = along(i, turned)
        out[i] = jnp.where(wall, m[i + 1], keep * m[i] + (rest + c_v))
        out[i + 1] = jnp.where(wall, m[i], keep * m[i + 1] + (rest - c_v))
    return out


def gradient(vector, density, plain, kind):
    inner = vector[0] * plain[0] + vector[1] * plain[1] + vector[2] * plain[2]
    return jnp.where(kind == 2, 0.0, rates(kind) * density * inner)


def kernel(
    sizes,
    forward_hbm,
    later_hbm,
    design_hbm,
    kind_hbm,
    region_hbm,
    adjoint_hbm,
    sensitivity_hbm,
    objective_ref,
    volumes_ref,
    forward,
    kind,
    region,
    pops,
    fields,
    macro,
    factors,
    grads,
    result,
    smooth,
    x_send,
    x_recv,
    y_send,
    y_recv,
    c_send,
    c_recv,
    stat_y,
    stat_x,
    load_sem,
    send_sem,
    recv_sem,
    sum_send,
    sum_recv,
):
    count_x, count_y = sizes
    nx, ny = kind.shape[0], kind.shape[1]
    me_x, me_y = lax.axis_index("gx"), lax.axis_index("gy")
    halves = range(0, ny, ROWS)

    def device(dx, dy):
        return (
            lax.rem(me_x + dx + count_x, count_x),
            lax.rem(me_y + dy + count_y, count_y),
        )

    def rim_planes(body, carry):
        return lax.fori_loop(0, 2, lambda k, c: body(k * (nx - 1), c), carry)

    def inner_planes(body, carry):
        return lax.fori_loop(1, nx - 1, body, carry)

    inner = (pl.ds(1, nx), pl.ds(ROWS, ny))
    loads = [
        pltpu.make_async_copy(
            design_hbm, fields.at[0, pl.ds(RAD, nx), pl.ds(ROWS, ny)], load_sem.at[0]
        ),
        pltpu.make_async_copy(later_hbm, pops.at[LATER, :, inner[0], inner[1]], load_sem.at[1]),
        pltpu.make_async_copy(forward_hbm, forward, load_sem.at[2]),
        pltpu.make_async_copy(kind_hbm, kind, load_sem.at[3]),
        pltpu.make_async_copy(region_hbm, region, load_sem.at[4]),
    ]
    for load in loads:
        load.start()

    partners = {((dx + count_x) % count_x, (dy + count_y) % count_y) for dx, dy in DIRS}
    partners |= {(0, k) for k in range(1, count_y)} | {(k, 0) for k in range(1, count_x)}
    barrier = pltpu.get_barrier_semaphore()
    for dx, dy in sorted(partners):
        pl.semaphore_signal(barrier, inc=1, device_id=device(dx, dy), device_id_type=MESH)
    loads[0].wait()
    pl.semaphore_wait(barrier, len(partners))

    def field_copies(slot, exchange):
        copies = []
        for j, (dx, dy) in enumerate(DIRS):
            width = nx if dx == 0 else RAD
            source_x = {0: RAD, 1: nx, -1: RAD}[dx]
            target_x = {0: RAD, 1: 0, -1: nx + RAD}[dx]
            height = ny if dy == 0 else ROWS
            source_y = {0: ROWS, 1: ny, -1: ROWS}[dy]
            target_y = {0: ROWS, 1: 0, -1: ny + ROWS}[dy]
            copies.append(
                pltpu.make_async_remote_copy(
                    src_ref=fields.at[slot, pl.ds(source_x, width), pl.ds(source_y, height)],
                    dst_ref=fields.at[slot, pl.ds(target_x, width), pl.ds(target_y, height)],
                    send_sem=send_sem.at[exchange, j],
                    recv_sem=recv_sem.at[exchange, j],
                    device_id=device(dx, dy),
                    device_id_type=MESH,
                )
            )
        return copies

    def pops_copies(slot):
        copies = []
        for j, direction in enumerate(DIRS):
            if direction[1] == 0:
                source, target, k = x_send, x_recv, j
            elif direction[0] == 0:
                source, target, k = y_send, y_recv, j - 2
            else:
                source, target, k = c_send, c_recv, j - 4
            copies.append(
                pltpu.make_async_remote_copy(
                    src_ref=source.at[slot, k],
                    dst_ref=target.at[slot, k],
                    send_sem=send_sem.at[slot, j],
                    recv_sem=recv_sem.at[slot, j],
                    device_id=device(*direction),
                    device_id_type=MESH,
                )
            )
        return copies

    def send_pops(slot, sign, copies, which):
        for j in which:
            dx, dy = DIRS[j]
            x = nx if dx == 1 else 1
            y = ROWS + ny - 1 if dy == 1 else ROWS
            for k, i in enumerate(crossing((dx, dy), sign)):
                if dy == 0:
                    x_send[slot, j, k] = pops[slot, i, x, ROWS : ROWS + ny, :]
                elif dx == 0:
                    for row in range(nx):
                        y_send[slot, j - 2, k, row : row + 1, :] = pops[
                            slot, i, row + 1, y : y + 1, :
                        ]
                else:
                    c_send[slot, j - 4] = pops[slot, i, x, y : y + 1, :]
            copies[j].start()

    def take_pops(slot, sign, copies, which):
        for j in which:
            dx, dy = DIRS[j]
            copies[j].wait_recv()
            x = 0 if dx == 1 else nx + 1
            y = ROWS - 1 if dy == 1 else ROWS + ny
            for k, i in enumerate(crossing((dx, dy), sign)):
                if dy == 0:
                    pops[slot, i, x, ROWS : ROWS + ny, :] = x_recv[slot, j, k]
                elif dx == 0:
                    for row in range(nx):
                        pops[slot, i, row + 1, y : y + 1, :] = y_recv[
                            slot, j - 2, k, row : row + 1, :
                        ]
                else:
                    pops[slot, i, x, y : y + 1, :] = c_recv[slot, j - 4]

    def pick(slot, i, x, y, sign):
        cx, cy, cz = (sign * c for c in VELOCITY[i])
        value = pops[slot, i, x + 1 + cx, ROWS + y + cy : 2 * ROWS + y + cy, :]
        return shifted(value, cz)

    design_copies = field_copies(0, DESIGN)
    for copy in design_copies:
        copy.start()
    loads[1].wait()
    later_copies = pops_copies(LATER)
    send_pops(LATER, -1, later_copies, ACROSS_X + ALONG_Y)
    for load in loads[2:]:
        load.wait()

    def macroscopic(x, carry):
        for y in halves:
            density, momenta = moments([forward[i, x, y : y + ROWS, :] for i in range(19)])
            inverse = 1.0 / density
            macro[0, x, y : y + ROWS, :] = density
            for a in range(3):
                macro[a + 1, x, y : y + ROWS, :] = momenta[a] * inverse
        return carry

    lax.fori_loop(0, nx, macroscopic, 0)
    inv_norm = inverse_norm((ROWS, kind.shape[2]))
    for copy in design_copies:
        copy.wait_recv()

    def first_step(x, sums):
        sums = list(sums)
        for y in halves:
            rows = slice(y, y + ROWS)
            kinds = kind[x, rows, :]
            design_cell = kinds == 1
            filtered = filter_taps(fields.at[0], x, y) * inv_norm
            factor = jnp.where(design_cell, 1.0 - BRINKMAN * (1.0 - filtered), 1.0)
            factors[x, rows, :] = factor
            regions = region[x, rows, :]
            inside = jnp.where(design_cell, filtered, 0.0)
            for r in range(REG):
                sums[r] = sums[r] + jnp.where(regions == r, inside, 0.0)
            post = collide(
                [forward[i, x, rows, :] for i in range(19)],
                macro[0, x, rows, :],
                [macro[a + 1, x, rows, :] for a in range(3)],
                kinds,
                factor,
            )
            for i in range(19):
                pops[POST, i, x + 1, ROWS + y : 2 * ROWS + y, :] = post[i]
        return tuple(sums)

    zero = jnp.zeros((ROWS, kind.shape[2]), jnp.float32)
    post_copies = pops_copies(POST)
    volumes = rim_planes(first_step, (zero,) * REG)
    send_pops(POST, 1, post_copies, ACROSS_X)
    volumes = inner_planes(first_step, volumes)
    send_pops(POST, 1, post_copies, ALONG_Y)
    take_pops(LATER, -1, later_copies, ALONG_Y + ACROSS_X)
    take_pops(POST, 1, post_copies, ALONG_Y)

    def middle_step(x, total):
        for y in halves:
            rows = slice(y, y + ROWS)
            kinds = kind[x, rows, :]
            factor = factors[x, rows, :]
            density, momenta = moments([pick(POST, i, x, y, -1) for i in range(19)])
            outlet = kinds == 4
            total = total + jnp.where(outlet, momenta[0], 0.0)
            inverse = 1.0 / density
            plain = [m * inverse for m in momenta]
            incoming = [pick(LATER, i, x, y, 1) for i in range(19)]
            rest, vector = adjoint_parts(incoming, plain, factor)
            grads[x, rows, :] = gradient(vector, density, plain, kinds)
            middle = adjoint_back(incoming, rest, vector, kinds, factor)
            source = jnp.where(outlet, 1.0, 0.0)
            for i in range(19):
                value = middle[i]
                if VELOCITY[i][0] == 1:
                    value = value + source
                elif VELOCITY[i][0] == -1:
                    value = value - source
                pops[MIDDLE, i, x + 1, ROWS + y : 2 * ROWS + y, :] = value
        return total

    objective = inner_planes(middle_step, zero)
    take_pops(POST, 1, post_copies, ACROSS_X)
    objective = rim_planes(middle_step, objective)
    middle_copies = pops_copies(MIDDLE)
    send_pops(MIDDLE, -1, middle_copies, ACROSS_X + ALONG_Y)

    def spread(stat, count, me, sem, place):
        copies = []
        for k in range(1, count):
            copies.append(
                pltpu.make_async_remote_copy(
                    src_ref=stat.at[me],
                    dst_ref=stat.at[me],
                    send_sem=sum_send.at[sem, k],
                    recv_sem=sum_recv.at[sem, k],
                    device_id=place(k),
                    device_id_type=MESH,
                )
            )
        for copy in copies:
            copy.start()
        return copies

    for r in range(REG):
        stat_y[me_y, r : r + 1, :] = jnp.sum(volumes[r], axis=0, keepdims=True)
    stat_y[me_y, REG : REG + 1, :] = jnp.sum(objective, axis=0, keepdims=True)
    stat_y[me_y, REG + 1 :, :] = jnp.zeros((REG - 1, zero.shape[1]), jnp.float32)
    sums_y = spread(stat_y, count_y, me_y, 0, lambda k: device(0, k))
    take_pops(MIDDLE, -1, middle_copies, ALONG_Y)

    def second_step(x, carry):
        for y in halves:
            rows = slice(y, y + ROWS)
            kinds = kind[x, rows, :]
            factor = factors[x, rows, :]
            density = macro[0, x, rows, :]
            plain = [macro[a + 1, x, rows, :] for a in range(3)]
            incoming = [pick(MIDDLE, i, x, y, 1) for i in range(19)]
            rest, vector = adjoint_parts(incoming, plain, factor)
            grad = grads[x, rows, :] + gradient(vector, density, plain, kinds)
            raw = jnp.where(kinds == 1, BRINKMAN * grad, 0.0) * inv_norm
            fields[1, x + RAD, ROWS + y : 2 * ROWS + y, :] = raw
            back = adjoint_back(incoming, rest, vector, kinds, factor)
            for i in range(19):
                result[i, x, rows, :] = back[i]
        return carry

    inner_planes(second_step, 0)
    take_pops(MIDDLE, -1, middle_copies, ACROSS_X)
    rim_planes(second_step, 0)
    raw_copies = field_copies(1, RAW)
    for copy in raw_copies:
        copy.start()
    store = pltpu.make_async_copy(result, adjoint_hbm, load_sem.at[5])
    store.start()

    for copy in sums_y:
        copy.wait()
    subtotal = stat_y[0]
    for k in range(1, count_y):
        subtotal = subtotal + stat_y[k]
    stat_x[me_x] = subtotal
    sums_x = spread(stat_x, count_x, me_x, 1, lambda k: device(k, 0))
    for copy in raw_copies:
        copy.wait_recv()

    def last_step(x, carry):
        for y in halves:
            smooth[x, y : y + ROWS, :] = filter_taps(fields.at[1], x, y)
        return carry

    lax.fori_loop(0, nx, last_step, 0)
    store_smooth = pltpu.make_async_copy(smooth, sensitivity_hbm, load_sem.at[6])
    store_smooth.start()
    for copy in sums_x:
        copy.wait()
    total = stat_x[0]
    for k in range(1, count_x):
        total = total + stat_x[k]
    total = jnp.sum(total, axis=1, keepdims=True)
    for r in range(REG):
        volumes_ref[r] = total[r, 0]
    objective_ref[0] = total[REG, 0]
    for copies in (design_copies, later_copies, post_copies, middle_copies, raw_copies):
        for copy in copies:
            copy.wait_send()
    store.wait()
    store_smooth.wait()


def per_device(sizes, forward_pops, later_adjoint, design, node_type, region):
    nx, ny, nz = design.shape
    f32 = jnp.float32
    anywhere = pl.BlockSpec(memory_space=pl.ANY)
    scalars = pl.BlockSpec(memory_space=pltpu.SMEM)
    block = (nx, ny, nz)
    most = max(sizes)
    adjoint, sensitivity, objective, volumes = pl.pallas_call(
        functools.partial(kernel, sizes),
        out_shape=(
            jax.ShapeDtypeStruct((19,) + block, f32),
            jax.ShapeDtypeStruct(block, f32),
            jax.ShapeDtypeStruct((1,), f32),
            jax.ShapeDtypeStruct((REG,), f32),
        ),
        in_specs=[anywhere] * 5,
        out_specs=(anywhere, anywhere, scalars, scalars),
        scratch_shapes=[
            pltpu.VMEM((19,) + block, f32),
            pltpu.VMEM(block, jnp.int32),
            pltpu.VMEM(block, jnp.int32),
            pltpu.VMEM((3, 19, nx + 2, ny + 2 * ROWS, nz), f32),
            pltpu.VMEM((2, nx + 2 * RAD, ny + 2 * ROWS, nz), f32),
            pltpu.VMEM((4,) + block, f32),
            pltpu.VMEM(block, f32),
            pltpu.VMEM(block, f32),
            pltpu.VMEM((19,) + block, f32),
            pltpu.VMEM(block, f32),
            pltpu.VMEM((3, 2, 5, ny, nz), f32),
            pltpu.VMEM((3, 2, 5, ny, nz), f32),
            pltpu.VMEM((3, 2, 5, nx, nz), f32),
            pltpu.VMEM((3, 2, 5, nx, nz), f32),
            pltpu.VMEM((3, 4, 1, nz), f32),
            pltpu.VMEM((3, 4, 1, nz), f32),
            pltpu.VMEM((sizes[1], 2 * REG, nz), f32),
            pltpu.VMEM((sizes[0], 2 * REG, nz), f32),
            pltpu.SemaphoreType.DMA((7,)),
            pltpu.SemaphoreType.DMA((5, 8)),
            pltpu.SemaphoreType.DMA((5, 8)),
            pltpu.SemaphoreType.DMA((2, most)),
            pltpu.SemaphoreType.DMA((2, most)),
        ],
        compiler_params=pltpu.CompilerParams(
            collective_id=0, has_side_effects=True, vmem_limit_bytes=60 * 1024 * 1024
        ),
        name="lattice_adjoint",
    )(forward_pops, later_adjoint, design, node_type, region)
    return adjoint, sensitivity, objective.reshape(()), volumes


def solution(mesh):
    sizes = (mesh.shape["gx"], mesh.shape["gy"])
    in_specs = (
        P(None, "gx", "gy", None),
        P(None, "gx", "gy", None),
        P("gx", "gy", None),
        P("gx", "gy", None),
        P("gx", "gy", None),
    )
    out_specs = (P(None, "gx", "gy", None), P("gx", "gy", None), P(), P())
    return jax.shard_map(
        functools.partial(per_device, sizes),
        mesh=mesh,
        in_specs=in_specs,
        out_specs=out_specs,
        check_vma=False,
    )
```

```python
import functools
import math

import jax
import jax.numpy as jnp
from jax import lax
from jax.experimental import pallas as pl
from jax.experimental.pallas import tpu as pltpu
from jax.sharding import PartitionSpec as P

RAD = 3
REG = 8
MESH = pl.DeviceIdType.MESH

VELOCITY = [
    (0, 0, 0),
    (1, 0, 0),
    (-1, 0, 0),
    (0, 1, 0),
    (0, -1, 0),
    (0, 0, 1),
    (0, 0, -1),
    (1, 1, 0),
    (-1, -1, 0),
    (1, -1, 0),
    (-1, 1, 0),
    (1, 0, 1),
    (-1, 0, -1),
    (1, 0, -1),
    (-1, 0, 1),
    (0, 1, 1),
    (0, -1, -1),
    (0, 1, -1),
    (0, -1, 1),
]
W0, W1, W2 = 1.0 / 3.0, 1.0 / 18.0, 1.0 / 36.0
PAIRS = [1, 3, 5, 7, 9, 11, 13, 15, 17]
OPPOSITE = [0, 2, 1, 4, 3, 6, 5, 8, 7, 10, 9, 12, 11, 14, 13, 16, 15, 18, 17]
RELAXATION = 1.0 / 0.6
BRINKMAN = 0.9

DIRS = [(1, 0), (-1, 0), (0, 1), (0, -1), (1, 1), (-1, -1), (1, -1), (-1, 1)]
ALONG_Y = [2, 3]
ACROSS_X = [0, 1, 4, 5, 6, 7]
ROWS = 8
POST, LATER, MIDDLE = 0, 1, 2
DESIGN, RAW = 3, 4


def weight(a, b, c):
    return max(RAD + 1 - math.sqrt(a * a + b * b + c * c), 0.0)


def crossing(direction, sign):
    return [
        i
        for i in range(19)
        if all(
            direction[a] == 0 or sign * VELOCITY[i][a] == direction[a] for a in range(2)
        )
    ]


def lanes(shape):
    return lax.broadcasted_iota(jnp.int32, shape, len(shape) - 1)


def shifted(value, offset):
    if offset == 0:
        return value
    depth = value.shape[-1]
    z = lanes(value.shape)
    rolled = pltpu.roll(value, (-offset) % depth, value.ndim - 1)
    inside = z < depth - offset if offset > 0 else z >= -offset
    return jnp.where(inside, rolled, 0.0)


def inverse_norm(shape):
    depth = shape[-1]
    z = lanes(shape)
    span = range(-RAD, RAD + 1)
    norm = jnp.zeros(shape, jnp.float32)
    for c in span:
        layer = sum(weight(a, b, c) for a in span for b in span)
        inside = (z + c >= 0) & (z + c < depth)
        norm = norm + jnp.where(inside, layer, 0.0)
    return 1.0 / norm


def filter_taps(field, x, y):
    classes = {}
    for a in range(-RAD, RAD + 1):
        for b in range(-RAD, RAD + 1):
            if weight(a, b, 0) > 0:
                value = field[x + RAD + a, ROWS + y + b : 2 * ROWS + y + b, :]
                key = a * a + b * b
                classes[key] = classes[key] + value if key in classes else value
    result = None
    for c in range(RAD + 1):
        layer = None
        for key, value in classes.items():
            w = max(RAD + 1 - math.sqrt(key + c * c), 0.0)
            if w > 0:
                layer = w * value if layer is None else layer + w * value
        if c == 0:
            result = layer
        else:
            result = result + shifted(layer, c) + shifted(layer, -c)
    return result


def pairs_of(p):
    return (
        {i: p[i] + p[i + 1] for i in PAIRS},
        {i: p[i] - p[i + 1] for i in PAIRS},
    )


def moments(p):
    even, odd = pairs_of(p)
    density = p[0] + (
        ((even[1] + even[3]) + (even[5] + even[7]))
        + ((even[9] + even[11]) + (even[13] + (even[15] + even[17])))
    )
    momenta = [
        (odd[1] + odd[7]) + (odd[9] + (odd[11] + odd[13])),
        (odd[3] + odd[7]) + (odd[15] + odd[17] - odd[9]),
        (odd[5] + odd[11]) + (odd[15] - odd[13] - odd[17]),
    ]
    return density, momenta


def along(i, u):
    total = None
    for a in range(3):
        if VELOCITY[i][a] != 0:
            if total is None:
                total = u[a]
            elif VELOCITY[i][a] > 0:
                total = total + u[a]
            else:
                total = total - u[a]
    return total


def rates(kind):
    return jnp.where(kind <= 1, RELAXATION, 1.0)


def collide(p, density, plain, kind, factor):
    u = [factor * v for v in plain]
    base = 1.0 - 1.5 * (u[0] * u[0] + u[1] * u[1] + u[2] * u[2])
    omega = rates(kind)
    keep = 1.0 - omega
    wall = kind == 2
    scale = omega * density
    scale1 = W1 * scale
    scale2 = W2 * scale
    out = [None] * 19
    out[0] = jnp.where(wall, p[0], keep * p[0] + (W0 * scale) * base)
    for i in PAIRS:
        c_u = along(i, u)
        s = scale1 if i < 7 else scale2
        even = s * (base + 4.5 * c_u * c_u)
        odd = s * (3.0 * c_u)
        out[i] = jnp.where(wall, p[i + 1], keep * p[i] + (even + odd))
        out[i + 1] = jnp.where(wall, p[i], keep * p[i + 1] + (even - odd))
    return out


def adjoint_parts(m, plain, factor):
    u = [factor * v for v in plain]
    even, odd = pairs_of(m)
    total = W0 * m[0] + W1 * (even[1] + even[3] + even[5])
    e79, e1113, e1517 = even[7] + even[9], even[11] + even[13], even[15] + even[17]
    total = total + W2 * (e79 + e1113 + e1517)
    first = [
        W1 * odd[1] + W2 * ((odd[7] + odd[9]) + (odd[11] + odd[13])),
        W1 * odd[3] + W2 * ((odd[7] - odd[9]) + (odd[15] + odd[17])),
        W1 * odd[5] + W2 * ((odd[11] - odd[13]) + (odd[15] - odd[17])),
    ]
    xx = W1 * even[1] + W2 * (e79 + e1113)
    yy = W1 * even[3] + W2 * (e79 + e1517)
    zz = W1 * even[5] + W2 * (e1113 + e1517)
    xy = W2 * (even[7] - even[9])
    xz = W2 * (even[11] - even[13])
    yz = W2 * (even[15] - even[17])
    second = [
        xx * u[0] + xy * u[1] + xz * u[2],
        xy * u[0] + yy * u[1] + yz * u[2],
        xz * u[0] + yz * u[1] + zz * u[2],
    ]

    def dot(p, q):
        return p[0] * q[0] + p[1] * q[1] + p[2] * q[2]

    scalar = total * (1.0 - 1.5 * dot(u, u)) + 3.0 * dot(u, first) + 4.5 * dot(u, second)
    vector = [3.0 * first[a] + 9.0 * second[a] - 3.0 * (u[a] * total) for a in range(3)]
    return scalar - dot(vector, u), vector


def adjoint_back(m, rest, vector, kind, factor):
    omega = rates(kind)
    keep = 1.0 - omega
    wall = kind == 2
    rest = omega * rest
    scale = omega * factor
    turned = [scale * v for v in vector]
    out = [None] * 19
    out[0] = jnp.where(wall, m[0], keep * m[0] + rest)
    for i in PAIRS:
        c_v = along(i, turned)
        out[i] = jnp.where(wall, m[i + 1], keep * m[i] + (rest + c_v))
        out[i + 1] = jnp.where(wall, m[i], keep * m[i + 1] + (rest - c_v))
    return out


def gradient(vector, density, plain, kind):
    inner = vector[0] * plain[0] + vector[1] * plain[1] + vector[2] * plain[2]
    return jnp.where(kind == 2, 0.0, rates(kind) * density * inner)


def kernel(
    sizes,
    forward_hbm,
    later_hbm,
    design_hbm,
    kind_hbm,
    region_hbm,
    adjoint_hbm,
    sensitivity_hbm,
    stats_ref,
    forward,
    kind,
    region,
    pops,
    fields,
    macro,
    factors,
    grads,
    result,
    smooth,
    x_send,
    x_recv,
    y_send,
    y_recv,
    c_send,
    c_recv,
    stat_y,
    stat_x,
    load_sem,
    send_sem,
    recv_sem,
    sum_send,
    sum_recv,
):
    count_x, count_y = sizes
    nx, ny = kind.shape[0], kind.shape[1]
    me_x, me_y = lax.axis_index("gx"), lax.axis_index("gy")
    halves = range(0, ny, ROWS)

    def device(dx, dy):
        return (
            lax.rem(me_x + dx + count_x, count_x),
            lax.rem(me_y + dy + count_y, count_y),
        )

    def rim_planes(body, carry):
        return lax.fori_loop(0, 2, lambda k, c: body(k * (nx - 1), c), carry)

    def inner_planes(body, carry):
        return lax.fori_loop(1, nx - 1, body, carry)

    inner = (pl.ds(1, nx), pl.ds(ROWS, ny))
    loads = [
        pltpu.make_async_copy(
            design_hbm, fields.at[0, pl.ds(RAD, nx), pl.ds(ROWS, ny)], load_sem.at[0]
        ),
        pltpu.make_async_copy(later_hbm, pops.at[LATER, :, inner[0], inner[1]], load_sem.at[1]),
        pltpu.make_async_copy(forward_hbm, forward, load_sem.at[2]),
        pltpu.make_async_copy(kind_hbm, kind, load_sem.at[3]),
        pltpu.make_async_copy(region_hbm, region, load_sem.at[4]),
    ]
    for load in loads:
        load.start()

    partners = {((dx + count_x) % count_x, (dy + count_y) % count_y) for dx, dy in DIRS}
    partners |= {(0, k) for k in range(1, count_y)} | {(k, 0) for k in range(1, count_x)}
    barrier = pltpu.get_barrier_semaphore()
    for dx, dy in sorted(partners):
        pl.semaphore_signal(barrier, inc=1, device_id=device(dx, dy), device_id_type=MESH)
    loads[0].wait()
    pl.semaphore_wait(barrier, len(partners))

    def field_copies(slot, exchange):
        copies = []
        for j, (dx, dy) in enumerate(DIRS):
            width = nx if dx == 0 else RAD
            source_x = {0: RAD, 1: nx, -1: RAD}[dx]
            target_x = {0: RAD, 1: 0, -1: nx + RAD}[dx]
            height = ny if dy == 0 else ROWS
            source_y = {0: ROWS, 1: ny, -1: ROWS}[dy]
            target_y = {0: ROWS, 1: 0, -1: ny + ROWS}[dy]
            copies.append(
                pltpu.make_async_remote_copy(
                    src_ref=fields.at[slot, pl.ds(source_x, width), pl.ds(source_y, height)],
                    dst_ref=fields.at[slot, pl.ds(target_x, width), pl.ds(target_y, height)],
                    send_sem=send_sem.at[exchange, j],
                    recv_sem=recv_sem.at[exchange, j],
                    device_id=device(dx, dy),
                    device_id_type=MESH,
                )
            )
        return copies

    def pops_copies(slot):
        copies = []
        for j, direction in enumerate(DIRS):
            if direction[1] == 0:
                source, target, k = x_send, x_recv, j
            elif direction[0] == 0:
                source, target, k = y_send, y_recv, j - 2
            else:
                source, target, k = c_send, c_recv, j - 4
            copies.append(
                pltpu.make_async_remote_copy(
                    src_ref=source.at[slot, k],
                    dst_ref=target.at[slot, k],
                    send_sem=send_sem.at[slot, j],
                    recv_sem=recv_sem.at[slot, j],
                    device_id=device(*direction),
                    device_id_type=MESH,
                )
            )
        return copies

    def send_pops(slot, sign, copies, which):
        for j in which:
            dx, dy = DIRS[j]
            x = nx if dx == 1 else 1
            y = ROWS + ny - 1 if dy == 1 else ROWS
            for k, i in enumerate(crossing((dx, dy), sign)):
                if dy == 0:
                    x_send[slot, j, k] = pops[slot, i, x, ROWS : ROWS + ny, :]
                elif dx == 0:
                    for row in range(nx):
                        y_send[slot, j - 2, k, row : row + 1, :] = pops[
                            slot, i, row + 1, y : y + 1, :
                        ]
                else:
                    c_send[slot, j - 4] = pops[slot, i, x, y : y + 1, :]
            copies[j].start()

    def take_pops(slot, sign, copies, which):
        for j in which:
            dx, dy = DIRS[j]
            copies[j].wait_recv()
            x = 0 if dx == 1 else nx + 1
            y = ROWS - 1 if dy == 1 else ROWS + ny
            for k, i in enumerate(crossing((dx, dy), sign)):
                if dy == 0:
                    pops[slot, i, x, ROWS : ROWS + ny, :] = x_recv[slot, j, k]
                elif dx == 0:
                    for row in range(nx):
                        pops[slot, i, row + 1, y : y + 1, :] = y_recv[
                            slot, j - 2, k, row : row + 1, :
                        ]
                else:
                    pops[slot, i, x, y : y + 1, :] = c_recv[slot, j - 4]

    def pick(slot, i, x, y, sign):
        cx, cy, cz = (sign * c for c in VELOCITY[i])
        value = pops[slot, i, x + 1 + cx, ROWS + y + cy : 2 * ROWS + y + cy, :]
        return shifted(value, cz)

    design_copies = field_copies(0, DESIGN)
    for copy in design_copies:
        copy.start()
    loads[1].wait()
    later_copies = pops_copies(LATER)
    send_pops(LATER, -1, later_copies, ACROSS_X + ALONG_Y)
    for load in loads[2:]:
        load.wait()

    def macroscopic(x, carry):
        for y in halves:
            density, momenta = moments([forward[i, x, y : y + ROWS, :] for i in range(19)])
            inverse = 1.0 / density
            macro[0, x, y : y + ROWS, :] = density
            for a in range(3):
                macro[a + 1, x, y : y + ROWS, :] = momenta[a] * inverse
        return carry

    lax.fori_loop(0, nx, macroscopic, 0)
    inv_norm = inverse_norm((ROWS, kind.shape[2]))
    for copy in design_copies:
        copy.wait_recv()

    def first_step(x, sums):
        sums = list(sums)
        for y in halves:
            rows = slice(y, y + ROWS)
            kinds = kind[x, rows, :]
            design_cell = kinds == 1
            filtered = filter_taps(fields.at[0], x, y) * inv_norm
            factor = jnp.where(design_cell, 1.0 - BRINKMAN * (1.0 - filtered), 1.0)
            factors[x, rows, :] = factor
            regions = region[x, rows, :]
            inside = jnp.where(design_cell, filtered, 0.0)
            for r in range(REG):
                sums[r] = sums[r] + jnp.where(regions == r, inside, 0.0)
            post = collide(
                [forward[i, x, rows, :] for i in range(19)],
                macro[0, x, rows, :],
                [macro[a + 1, x, rows, :] for a in range(3)],
                kinds,
                factor,
            )
            for i in range(19):
                pops[POST, i, x + 1, ROWS + y : 2 * ROWS + y, :] = post[i]
        return tuple(sums)

    zero = jnp.zeros((ROWS, kind.shape[2]), jnp.float32)
    post_copies = pops_copies(POST)
    volumes = rim_planes(first_step, (zero,) * REG)
    send_pops(POST, 1, post_copies, ACROSS_X)
    volumes = inner_planes(first_step, volumes)
    send_pops(POST, 1, post_copies, ALONG_Y)
    take_pops(LATER, -1, later_copies, ALONG_Y + ACROSS_X)
    take_pops(POST, 1, post_copies, ALONG_Y)

    def middle_step(x, total):
        for y in halves:
            rows = slice(y, y + ROWS)
            kinds = kind[x, rows, :]
            factor = factors[x, rows, :]
            density, momenta = moments([pick(POST, i, x, y, -1) for i in range(19)])
            outlet = kinds == 4
            total = total + jnp.where(outlet, momenta[0], 0.0)
            inverse = 1.0 / density
            plain = [m * inverse for m in momenta]
            incoming = [pick(LATER, i, x, y, 1) for i in range(19)]
            rest, vector = adjoint_parts(incoming, plain, factor)
            grads[x, rows, :] = gradient(vector, density, plain, kinds)
            middle = adjoint_back(incoming, rest, vector, kinds, factor)
            source = jnp.where(outlet, 1.0, 0.0)
            for i in range(19):
                value = middle[i]
                if VELOCITY[i][0] == 1:
                    value = value + source
                elif VELOCITY[i][0] == -1:
                    value = value - source
                pops[MIDDLE, i, x + 1, ROWS + y : 2 * ROWS + y, :] = value
        return total

    objective = inner_planes(middle_step, zero)
    take_pops(POST, 1, post_copies, ACROSS_X)
    objective = rim_planes(middle_step, objective)
    middle_copies = pops_copies(MIDDLE)
    send_pops(MIDDLE, -1, middle_copies, ACROSS_X + ALONG_Y)

    def spread(stat, count, me, sem, place):
        copies = []
        for k in range(1, count):
            copies.append(
                pltpu.make_async_remote_copy(
                    src_ref=stat.at[me],
                    dst_ref=stat.at[me],
                    send_sem=sum_send.at[sem, k],
                    recv_sem=sum_recv.at[sem, k],
                    device_id=place(k),
                    device_id_type=MESH,
                )
            )
        for copy in copies:
            copy.start()
        return copies

    for r in range(REG):
        stat_y[me_y, r : r + 1, :] = jnp.sum(volumes[r], axis=0, keepdims=True)
    stat_y[me_y, REG : REG + 1, :] = jnp.sum(objective, axis=0, keepdims=True)
    stat_y[me_y, REG + 1 :, :] = jnp.zeros((REG - 1, zero.shape[1]), jnp.float32)
    sums_y = spread(stat_y, count_y, me_y, 0, lambda k: device(0, k))
    take_pops(MIDDLE, -1, middle_copies, ALONG_Y)

    def second_step(x, carry):
        for y in halves:
            rows = slice(y, y + ROWS)
            kinds = kind[x, rows, :]
            factor = factors[x, rows, :]
            density = macro[0, x, rows, :]
            plain = [macro[a + 1, x, rows, :] for a in range(3)]
            incoming = [pick(MIDDLE, i, x, y, 1) for i in range(19)]
            rest, vector = adjoint_parts(incoming, plain, factor)
            grad = grads[x, rows, :] + gradient(vector, density, plain, kinds)
            raw = jnp.where(kinds == 1, BRINKMAN * grad, 0.0) * inv_norm
            fields[1, x + RAD, ROWS + y : 2 * ROWS + y, :] = raw
            back = adjoint_back(incoming, rest, vector, kinds, factor)
            for i in range(19):
                result[i, x, rows, :] = back[i]
        return carry

    inner_planes(second_step, 0)
    take_pops(MIDDLE, -1, middle_copies, ACROSS_X)
    rim_planes(second_step, 0)
    raw_copies = field_copies(1, RAW)
    for copy in raw_copies:
        copy.start()
    store = pltpu.make_async_copy(result, adjoint_hbm, load_sem.at[5])
    store.start()

    for copy in sums_y:
        copy.wait()
    subtotal = stat_y[0]
    for k in range(1, count_y):
        subtotal = subtotal + stat_y[k]
    stat_x[me_x] = subtotal
    sums_x = spread(stat_x, count_x, me_x, 1, lambda k: device(k, 0))
    for copy in raw_copies:
        copy.wait_recv()

    def last_step(x, carry):
        for y in halves:
            smooth[x, y : y + ROWS, :] = filter_taps(fields.at[1], x, y)
        return carry

    lax.fori_loop(0, nx, last_step, 0)
    store_smooth = pltpu.make_async_copy(smooth, sensitivity_hbm, load_sem.at[6])
    store_smooth.start()
    for copy in sums_x:
        copy.wait()
    total = stat_x[0]
    for k in range(1, count_x):
        total = total + stat_x[k]
    stats_ref[...] = total
    for copies in (design_copies, later_copies, post_copies, middle_copies, raw_copies):
        for copy in copies:
            copy.wait_send()
    store.wait()
    store_smooth.wait()


def finish(
    adjoint_in,
    sensitivity_in,
    stats_in,
    adjoint_out,
    sensitivity_out,
    objective_ref,
    volumes_ref,
    stats,
    sem,
):
    load = pltpu.make_async_copy(stats_in, stats, sem.at[0])
    load.start()
    count = adjoint_in.shape[0]
    copies = [
        pltpu.make_async_copy(adjoint_in.at[i], adjoint_out.at[i], sem.at[2 + i])
        for i in range(count)
    ]
    copies.append(pltpu.make_async_copy(sensitivity_in, sensitivity_out, sem.at[1]))
    for copy in copies:
        copy.start()
    load.wait()
    total = jnp.sum(stats[...], axis=1, keepdims=True)
    for r in range(REG):
        volumes_ref[r] = total[r, 0]
    objective_ref[0] = total[REG, 0]
    for copy in copies:
        copy.wait()


def per_device(sizes, forward_pops, later_adjoint, design, node_type, region):
    nx, ny, nz = design.shape
    f32 = jnp.float32
    anywhere = pl.BlockSpec(memory_space=pl.ANY)
    scalars = pl.BlockSpec(memory_space=pltpu.SMEM)
    block = (nx, ny, nz)
    most = max(sizes)
    adjoint, sensitivity, stats = pl.pallas_call(
        functools.partial(kernel, sizes),
        out_shape=(
            jax.ShapeDtypeStruct((19,) + block, f32),
            jax.ShapeDtypeStruct(block, f32),
            jax.ShapeDtypeStruct((2 * REG, nz), f32),
        ),
        in_specs=[anywhere] * 5,
        out_specs=(anywhere, anywhere, pl.BlockSpec(memory_space=pltpu.VMEM)),
        scratch_shapes=[
            pltpu.VMEM((19,) + block, f32),
            pltpu.VMEM(block, jnp.int32),
            pltpu.VMEM(block, jnp.int32),
            pltpu.VMEM((3, 19, nx + 2, ny + 2 * ROWS, nz), f32),
            pltpu.VMEM((2, nx + 2 * RAD, ny + 2 * ROWS, nz), f32),
            pltpu.VMEM((4,) + block, f32),
            pltpu.VMEM(block, f32),
            pltpu.VMEM(block, f32),
            pltpu.VMEM((19,) + block, f32),
            pltpu.VMEM(block, f32),
            pltpu.VMEM((3, 2, 5, ny, nz), f32),
            pltpu.VMEM((3, 2, 5, ny, nz), f32),
            pltpu.VMEM((3, 2, 5, nx, nz), f32),
            pltpu.VMEM((3, 2, 5, nx, nz), f32),
            pltpu.VMEM((3, 4, 1, nz), f32),
            pltpu.VMEM((3, 4, 1, nz), f32),
            pltpu.VMEM((sizes[1], 2 * REG, nz), f32),
            pltpu.VMEM((sizes[0], 2 * REG, nz), f32),
            pltpu.SemaphoreType.DMA((7,)),
            pltpu.SemaphoreType.DMA((5, 8)),
            pltpu.SemaphoreType.DMA((5, 8)),
            pltpu.SemaphoreType.DMA((2, most)),
            pltpu.SemaphoreType.DMA((2, most)),
        ],
        compiler_params=pltpu.CompilerParams(
            collective_id=0, has_side_effects=True, vmem_limit_bytes=60 * 1024 * 1024
        ),
        name="lattice_adjoint",
    )(forward_pops, later_adjoint, design, node_type, region)
    adjoint, sensitivity, objective, volumes = pl.pallas_call(
        finish,
        out_shape=(
            jax.ShapeDtypeStruct((19,) + block, f32),
            jax.ShapeDtypeStruct(block, f32),
            jax.ShapeDtypeStruct((1,), f32),
            jax.ShapeDtypeStruct((REG,), f32),
        ),
        in_specs=[anywhere] * 3,
        out_specs=(anywhere, anywhere, scalars, scalars),
        scratch_shapes=[
            pltpu.VMEM((2 * REG, nz), f32),
            pltpu.SemaphoreType.DMA((21,)),
        ],
        compiler_params=pltpu.CompilerParams(vmem_limit_bytes=60 * 1024 * 1024),
        name="place_results",
    )(adjoint, sensitivity, stats)
    return adjoint, sensitivity, objective.reshape(()), volumes


def solution(mesh):
    sizes = (mesh.shape["gx"], mesh.shape["gy"])
    in_specs = (
        P(None, "gx", "gy", None),
        P(None, "gx", "gy", None),
        P("gx", "gy", None),
        P("gx", "gy", None),
        P("gx", "gy", None),
    )
    out_specs = (P(None, "gx", "gy", None), P("gx", "gy", None), P(), P())
    return jax.shard_map(
        functools.partial(per_device, sizes),
        mesh=mesh,
        in_specs=in_specs,
        out_specs=out_specs,
        check_vma=False,
    )
```

```python
import functools
import math

import jax
import jax.numpy as jnp
from jax import lax
from jax.experimental import pallas as pl
from jax.experimental.pallas import tpu as pltpu
from jax.sharding import PartitionSpec as P

RAD = 3
REG = 8
MESH = pl.DeviceIdType.MESH

VELOCITY = [
    (0, 0, 0),
    (1, 0, 0),
    (-1, 0, 0),
    (0, 1, 0),
    (0, -1, 0),
    (0, 0, 1),
    (0, 0, -1),
    (1, 1, 0),
    (-1, -1, 0),
    (1, -1, 0),
    (-1, 1, 0),
    (1, 0, 1),
    (-1, 0, -1),
    (1, 0, -1),
    (-1, 0, 1),
    (0, 1, 1),
    (0, -1, -1),
    (0, 1, -1),
    (0, -1, 1),
]
W0, W1, W2 = 1.0 / 3.0, 1.0 / 18.0, 1.0 / 36.0
PAIRS = [1, 3, 5, 7, 9, 11, 13, 15, 17]
OPPOSITE = [0, 2, 1, 4, 3, 6, 5, 8, 7, 10, 9, 12, 11, 14, 13, 16, 15, 18, 17]
RELAXATION = 1.0 / 0.6
BRINKMAN = 0.9

DIRS = [(1, 0), (-1, 0), (0, 1), (0, -1), (1, 1), (-1, -1), (1, -1), (-1, 1)]
ALONG_Y = [2, 3]
ACROSS_X = [0, 1, 4, 5, 6, 7]
ROWS = 8
POST, LATER, MIDDLE = 0, 1, 2
DESIGN, RAW = 3, 4


def weight(a, b, c):
    return max(RAD + 1 - math.sqrt(a * a + b * b + c * c), 0.0)


def crossing(direction, sign):
    return [
        i
        for i in range(19)
        if all(
            direction[a] == 0 or sign * VELOCITY[i][a] == direction[a] for a in range(2)
        )
    ]


def lanes(shape):
    return lax.broadcasted_iota(jnp.int32, shape, len(shape) - 1)


def shifted(value, offset):
    if offset == 0:
        return value
    depth = value.shape[-1]
    z = lanes(value.shape)
    rolled = pltpu.roll(value, (-offset) % depth, value.ndim - 1)
    inside = z < depth - offset if offset > 0 else z >= -offset
    return jnp.where(inside, rolled, 0.0)


def inverse_norm(shape):
    depth = shape[-1]
    z = lanes(shape)
    span = range(-RAD, RAD + 1)
    norm = jnp.zeros(shape, jnp.float32)
    for c in span:
        layer = sum(weight(a, b, c) for a in span for b in span)
        inside = (z + c >= 0) & (z + c < depth)
        norm = norm + jnp.where(inside, layer, 0.0)
    return 1.0 / norm


def filter_taps(field, x, y):
    classes = {}
    for a in range(-RAD, RAD + 1):
        for b in range(-RAD, RAD + 1):
            if weight(a, b, 0) > 0:
                value = field[x + RAD + a, ROWS + y + b : 2 * ROWS + y + b, :]
                key = a * a + b * b
                classes[key] = classes[key] + value if key in classes else value
    result = None
    for c in range(RAD + 1):
        layer = None
        for key, value in classes.items():
            w = max(RAD + 1 - math.sqrt(key + c * c), 0.0)
            if w > 0:
                layer = w * value if layer is None else layer + w * value
        if c == 0:
            result = layer
        else:
            result = result + shifted(layer, c) + shifted(layer, -c)
    return result


def pairs_of(p):
    return (
        {i: p[i] + p[i + 1] for i in PAIRS},
        {i: p[i] - p[i + 1] for i in PAIRS},
    )


def moments(p):
    even, odd = pairs_of(p)
    density = p[0] + (
        ((even[1] + even[3]) + (even[5] + even[7]))
        + ((even[9] + even[11]) + (even[13] + (even[15] + even[17])))
    )
    momenta = [
        (odd[1] + odd[7]) + (odd[9] + (odd[11] + odd[13])),
        (odd[3] + odd[7]) + (odd[15] + odd[17] - odd[9]),
        (odd[5] + odd[11]) + (odd[15] - odd[13] - odd[17]),
    ]
    return density, momenta


def along(i, u):
    total = None
    for a in range(3):
        if VELOCITY[i][a] != 0:
            if total is None:
                total = u[a]
            elif VELOCITY[i][a] > 0:
                total = total + u[a]
            else:
                total = total - u[a]
    return total


def rates(kind):
    return jnp.where(kind <= 1, RELAXATION, 1.0)


def collide(p, density, plain, kind, factor):
    u = [factor * v for v in plain]
    base = 1.0 - 1.5 * (u[0] * u[0] + u[1] * u[1] + u[2] * u[2])
    omega = rates(kind)
    keep = 1.0 - omega
    wall = kind == 2
    scale = omega * density
    scale1 = W1 * scale
    scale2 = W2 * scale
    out = [None] * 19
    out[0] = jnp.where(wall, p[0], keep * p[0] + (W0 * scale) * base)
    for i in PAIRS:
        c_u = along(i, u)
        s = scale1 if i < 7 else scale2
        even = s * (base + 4.5 * c_u * c_u)
        odd = s * (3.0 * c_u)
        out[i] = jnp.where(wall, p[i + 1], keep * p[i] + (even + odd))
        out[i + 1] = jnp.where(wall, p[i], keep * p[i + 1] + (even - odd))
    return out


def adjoint_parts(m, plain, factor):
    u = [factor * v for v in plain]
    even, odd = pairs_of(m)
    total = W0 * m[0] + W1 * (even[1] + even[3] + even[5])
    e79, e1113, e1517 = even[7] + even[9], even[11] + even[13], even[15] + even[17]
    total = total + W2 * (e79 + e1113 + e1517)
    first = [
        W1 * odd[1] + W2 * ((odd[7] + odd[9]) + (odd[11] + odd[13])),
        W1 * odd[3] + W2 * ((odd[7] - odd[9]) + (odd[15] + odd[17])),
        W1 * odd[5] + W2 * ((odd[11] - odd[13]) + (odd[15] - odd[17])),
    ]
    xx = W1 * even[1] + W2 * (e79 + e1113)
    yy = W1 * even[3] + W2 * (e79 + e1517)
    zz = W1 * even[5] + W2 * (e1113 + e1517)
    xy = W2 * (even[7] - even[9])
    xz = W2 * (even[11] - even[13])
    yz = W2 * (even[15] - even[17])
    second = [
        xx * u[0] + xy * u[1] + xz * u[2],
        xy * u[0] + yy * u[1] + yz * u[2],
        xz * u[0] + yz * u[1] + zz * u[2],
    ]

    def dot(p, q):
        return p[0] * q[0] + p[1] * q[1] + p[2] * q[2]

    scalar = total * (1.0 - 1.5 * dot(u, u)) + 3.0 * dot(u, first) + 4.5 * dot(u, second)
    vector = [3.0 * first[a] + 9.0 * second[a] - 3.0 * (u[a] * total) for a in range(3)]
    return scalar - dot(vector, u), vector


def adjoint_back(m, rest, vector, kind, factor):
    omega = rates(kind)
    keep = 1.0 - omega
    wall = kind == 2
    rest = omega * rest
    scale = omega * factor
    turned = [scale * v for v in vector]
    out = [None] * 19
    out[0] = jnp.where(wall, m[0], keep * m[0] + rest)
    for i in PAIRS:
        c_v = along(i, turned)
        out[i] = jnp.where(wall, m[i + 1], keep * m[i] + (rest + c_v))
        out[i + 1] = jnp.where(wall, m[i], keep * m[i + 1] + (rest - c_v))
    return out


def gradient(vector, density, plain, kind):
    inner = vector[0] * plain[0] + vector[1] * plain[1] + vector[2] * plain[2]
    return jnp.where(kind == 2, 0.0, rates(kind) * density * inner)


def kernel(
    sizes,
    forward_hbm,
    later_hbm,
    design_hbm,
    kind_hbm,
    region_hbm,
    adjoint_hbm,
    sensitivity_hbm,
    stats_ref,
    forward,
    kind,
    region,
    pops,
    fields,
    macro,
    factors,
    grads,
    result,
    smooth,
    x_send,
    x_recv,
    y_send,
    y_recv,
    c_send,
    c_recv,
    stat_y,
    stat_x,
    load_sem,
    send_sem,
    recv_sem,
    sum_send,
    sum_recv,
):
    count_x, count_y = sizes
    nx, ny = kind.shape[0], kind.shape[1]
    me_x, me_y = lax.axis_index("gx"), lax.axis_index("gy")
    halves = range(0, ny, ROWS)

    def device(dx, dy):
        return (
            lax.rem(me_x + dx + count_x, count_x),
            lax.rem(me_y + dy + count_y, count_y),
        )

    def rim_planes(body, carry):
        return lax.fori_loop(0, 2, lambda k, c: body(k * (nx - 1), c), carry)

    def inner_planes(body, carry):
        return lax.fori_loop(1, nx - 1, body, carry)

    inner = (pl.ds(1, nx), pl.ds(ROWS, ny))
    loads = [
        pltpu.make_async_copy(
            design_hbm, fields.at[0, pl.ds(RAD, nx), pl.ds(ROWS, ny)], load_sem.at[0]
        ),
        pltpu.make_async_copy(later_hbm, pops.at[LATER, :, inner[0], inner[1]], load_sem.at[1]),
        pltpu.make_async_copy(forward_hbm, forward, load_sem.at[2]),
        pltpu.make_async_copy(kind_hbm, kind, load_sem.at[3]),
        pltpu.make_async_copy(region_hbm, region, load_sem.at[4]),
    ]
    for load in loads:
        load.start()

    partners = {((dx + count_x) % count_x, (dy + count_y) % count_y) for dx, dy in DIRS}
    partners |= {(0, k) for k in range(1, count_y)} | {(k, 0) for k in range(1, count_x)}
    barrier = pltpu.get_barrier_semaphore()
    for dx, dy in sorted(partners):
        pl.semaphore_signal(barrier, inc=1, device_id=device(dx, dy), device_id_type=MESH)
    loads[0].wait()
    pl.semaphore_wait(barrier, len(partners))

    def field_copies(slot, exchange):
        copies = []
        for j, (dx, dy) in enumerate(DIRS):
            width = nx if dx == 0 else RAD
            source_x = {0: RAD, 1: nx, -1: RAD}[dx]
            target_x = {0: RAD, 1: 0, -1: nx + RAD}[dx]
            height = ny if dy == 0 else ROWS
            source_y = {0: ROWS, 1: ny, -1: ROWS}[dy]
            target_y = {0: ROWS, 1: 0, -1: ny + ROWS}[dy]
            copies.append(
                pltpu.make_async_remote_copy(
                    src_ref=fields.at[slot, pl.ds(source_x, width), pl.ds(source_y, height)],
                    dst_ref=fields.at[slot, pl.ds(target_x, width), pl.ds(target_y, height)],
                    send_sem=send_sem.at[exchange, j],
                    recv_sem=recv_sem.at[exchange, j],
                    device_id=device(dx, dy),
                    device_id_type=MESH,
                )
            )
        return copies

    def pops_copies(slot):
        copies = []
        for j, direction in enumerate(DIRS):
            if direction[1] == 0:
                source, target, k = x_send, x_recv, j
            elif direction[0] == 0:
                source, target, k = y_send, y_recv, j - 2
            else:
                source, target, k = c_send, c_recv, j - 4
            copies.append(
                pltpu.make_async_remote_copy(
                    src_ref=source.at[slot, k],
                    dst_ref=target.at[slot, k],
                    send_sem=send_sem.at[slot, j],
                    recv_sem=recv_sem.at[slot, j],
                    device_id=device(*direction),
                    device_id_type=MESH,
                )
            )
        return copies

    def send_pops(slot, sign, copies, which):
        for j in which:
            dx, dy = DIRS[j]
            x = nx if dx == 1 else 1
            y = ROWS + ny - 1 if dy == 1 else ROWS
            for k, i in enumerate(crossing((dx, dy), sign)):
                if dy == 0:
                    x_send[slot, j, k] = pops[slot, i, x, ROWS : ROWS + ny, :]
                elif dx == 0:
                    for row in range(nx):
                        y_send[slot, j - 2, k, row : row + 1, :] = pops[
                            slot, i, row + 1, y : y + 1, :
                        ]
                else:
                    c_send[slot, j - 4] = pops[slot, i, x, y : y + 1, :]
            copies[j].start()

    def take_pops(slot, sign, copies, which):
        for j in which:
            dx, dy = DIRS[j]
            copies[j].wait_recv()
            x = 0 if dx == 1 else nx + 1
            y = ROWS - 1 if dy == 1 else ROWS + ny
            for k, i in enumerate(crossing((dx, dy), sign)):
                if dy == 0:
                    pops[slot, i, x, ROWS : ROWS + ny, :] = x_recv[slot, j, k]
                elif dx == 0:
                    for row in range(nx):
                        pops[slot, i, row + 1, y : y + 1, :] = y_recv[
                            slot, j - 2, k, row : row + 1, :
                        ]
                else:
                    pops[slot, i, x, y : y + 1, :] = c_recv[slot, j - 4]

    def pick(slot, i, x, y, sign):
        cx, cy, cz = (sign * c for c in VELOCITY[i])
        value = pops[slot, i, x + 1 + cx, ROWS + y + cy : 2 * ROWS + y + cy, :]
        return shifted(value, cz)

    design_copies = field_copies(0, DESIGN)
    for copy in design_copies:
        copy.start()
    loads[1].wait()
    later_copies = pops_copies(LATER)
    send_pops(LATER, -1, later_copies, ACROSS_X + ALONG_Y)
    for load in loads[2:]:
        load.wait()

    def macroscopic(x, carry):
        for y in halves:
            density, momenta = moments([forward[i, x, y : y + ROWS, :] for i in range(19)])
            inverse = 1.0 / density
            macro[0, x, y : y + ROWS, :] = density
            for a in range(3):
                macro[a + 1, x, y : y + ROWS, :] = momenta[a] * inverse
        return carry

    lax.fori_loop(0, nx, macroscopic, 0)
    inv_norm = inverse_norm((ROWS, kind.shape[2]))
    for copy in design_copies:
        copy.wait_recv()

    def first_step(x, sums):
        sums = list(sums)
        for y in halves:
            rows = slice(y, y + ROWS)
            kinds = kind[x, rows, :]
            design_cell = kinds == 1
            filtered = filter_taps(fields.at[0], x, y) * inv_norm
            factor = jnp.where(design_cell, 1.0 - BRINKMAN * (1.0 - filtered), 1.0)
            factors[x, rows, :] = factor
            regions = region[x, rows, :]
            inside = jnp.where(design_cell, filtered, 0.0)
            for r in range(REG):
                sums[r] = sums[r] + jnp.where(regions == r, inside, 0.0)
            post = collide(
                [forward[i, x, rows, :] for i in range(19)],
                macro[0, x, rows, :],
                [macro[a + 1, x, rows, :] for a in range(3)],
                kinds,
                factor,
            )
            for i in range(19):
                pops[POST, i, x + 1, ROWS + y : 2 * ROWS + y, :] = post[i]
        return tuple(sums)

    zero = jnp.zeros((ROWS, kind.shape[2]), jnp.float32)
    post_copies = pops_copies(POST)
    volumes = rim_planes(first_step, (zero,) * REG)
    send_pops(POST, 1, post_copies, ACROSS_X)
    volumes = inner_planes(first_step, volumes)
    send_pops(POST, 1, post_copies, ALONG_Y)
    take_pops(LATER, -1, later_copies, ALONG_Y + ACROSS_X)
    take_pops(POST, 1, post_copies, ALONG_Y)

    def middle_step(x, total):
        for y in halves:
            rows = slice(y, y + ROWS)
            kinds = kind[x, rows, :]
            factor = factors[x, rows, :]
            density, momenta = moments([pick(POST, i, x, y, -1) for i in range(19)])
            outlet = kinds == 4
            total = total + jnp.where(outlet, momenta[0], 0.0)
            inverse = 1.0 / density
            plain = [m * inverse for m in momenta]
            incoming = [pick(LATER, i, x, y, 1) for i in range(19)]
            rest, vector = adjoint_parts(incoming, plain, factor)
            grads[x, rows, :] = gradient(vector, density, plain, kinds)
            middle = adjoint_back(incoming, rest, vector, kinds, factor)
            source = jnp.where(outlet, 1.0, 0.0)
            for i in range(19):
                value = middle[i]
                if VELOCITY[i][0] == 1:
                    value = value + source
                elif VELOCITY[i][0] == -1:
                    value = value - source
                pops[MIDDLE, i, x + 1, ROWS + y : 2 * ROWS + y, :] = value
        return total

    objective = inner_planes(middle_step, zero)
    take_pops(POST, 1, post_copies, ACROSS_X)
    objective = rim_planes(middle_step, objective)
    middle_copies = pops_copies(MIDDLE)
    send_pops(MIDDLE, -1, middle_copies, ACROSS_X + ALONG_Y)

    def spread(stat, count, me, sem, place):
        copies = []
        for k in range(1, count):
            copies.append(
                pltpu.make_async_remote_copy(
                    src_ref=stat.at[me],
                    dst_ref=stat.at[me],
                    send_sem=sum_send.at[sem, k],
                    recv_sem=sum_recv.at[sem, k],
                    device_id=place(k),
                    device_id_type=MESH,
                )
            )
        for copy in copies:
            copy.start()
        return copies

    for r in range(REG):
        stat_y[me_y, r : r + 1, :] = jnp.sum(volumes[r], axis=0, keepdims=True)
    stat_y[me_y, REG : REG + 1, :] = jnp.sum(objective, axis=0, keepdims=True)
    stat_y[me_y, REG + 1 :, :] = jnp.zeros((REG - 1, zero.shape[1]), jnp.float32)
    sums_y = spread(stat_y, count_y, me_y, 0, lambda k: device(0, k))
    take_pops(MIDDLE, -1, middle_copies, ALONG_Y)

    def second_step(x, carry):
        for y in halves:
            rows = slice(y, y + ROWS)
            kinds = kind[x, rows, :]
            factor = factors[x, rows, :]
            density = macro[0, x, rows, :]
            plain = [macro[a + 1, x, rows, :] for a in range(3)]
            incoming = [pick(MIDDLE, i, x, y, 1) for i in range(19)]
            rest, vector = adjoint_parts(incoming, plain, factor)
            grad = grads[x, rows, :] + gradient(vector, density, plain, kinds)
            raw = jnp.where(kinds == 1, BRINKMAN * grad, 0.0) * inv_norm
            fields[1, x + RAD, ROWS + y : 2 * ROWS + y, :] = raw
            back = adjoint_back(incoming, rest, vector, kinds, factor)
            for i in range(19):
                result[i, x, rows, :] = back[i]
        return carry

    inner_planes(second_step, 0)
    take_pops(MIDDLE, -1, middle_copies, ACROSS_X)
    rim_planes(second_step, 0)
    raw_copies = field_copies(1, RAW)
    for copy in raw_copies:
        copy.start()
    store = pltpu.make_async_copy(result, adjoint_hbm, load_sem.at[5])
    store.start()

    for copy in sums_y:
        copy.wait()
    subtotal = stat_y[0]
    for k in range(1, count_y):
        subtotal = subtotal + stat_y[k]
    stat_x[me_x] = subtotal
    sums_x = spread(stat_x, count_x, me_x, 1, lambda k: device(k, 0))
    for copy in raw_copies:
        copy.wait_recv()

    def last_step(x, carry):
        for y in halves:
            smooth[x, y : y + ROWS, :] = filter_taps(fields.at[1], x, y)
        return carry

    lax.fori_loop(0, nx, last_step, 0)
    store_smooth = pltpu.make_async_copy(smooth, sensitivity_hbm, load_sem.at[6])
    store_smooth.start()
    for copy in sums_x:
        copy.wait()
    total = stat_x[0]
    for k in range(1, count_x):
        total = total + stat_x[k]
    stats_ref[...] = total
    for copies in (design_copies, later_copies, post_copies, middle_copies, raw_copies):
        for copy in copies:
            copy.wait_send()
    store.wait()
    store_smooth.wait()


def finish(
    adjoint_in,
    sensitivity_in,
    stats_in,
    adjoint_out,
    sensitivity_out,
    objective_ref,
    volumes_ref,
    stats,
    held,
    smooth,
    sem,
):
    load = pltpu.make_async_copy(stats_in, stats, sem.at[0])
    load.start()
    ways = [(adjoint_in.at[i], held.at[i], adjoint_out.at[i]) for i in range(19)]
    ways.append((sensitivity_in, smooth, sensitivity_out))
    loads = [
        pltpu.make_async_copy(way[0], way[1], sem.at[1 + k])
        for k, way in enumerate(ways)
    ]
    copies = [
        pltpu.make_async_copy(way[1], way[2], sem.at[21 + k])
        for k, way in enumerate(ways)
    ]
    for copy in loads:
        copy.start()
    for arrival, copy in zip(loads, copies):
        arrival.wait()
        copy.start()
    load.wait()
    total = jnp.sum(stats[...], axis=1, keepdims=True)
    for r in range(REG):
        volumes_ref[r] = total[r, 0]
    objective_ref[0] = total[REG, 0]
    for copy in copies:
        copy.wait()


def per_device(sizes, forward_pops, later_adjoint, design, node_type, region):
    nx, ny, nz = design.shape
    f32 = jnp.float32
    anywhere = pl.BlockSpec(memory_space=pl.ANY)
    scalars = pl.BlockSpec(memory_space=pltpu.SMEM)
    block = (nx, ny, nz)
    most = max(sizes)
    adjoint, sensitivity, stats = pl.pallas_call(
        functools.partial(kernel, sizes),
        out_shape=(
            jax.ShapeDtypeStruct((19,) + block, f32),
            jax.ShapeDtypeStruct(block, f32),
            jax.ShapeDtypeStruct((2 * REG, nz), f32),
        ),
        in_specs=[anywhere] * 5,
        out_specs=(anywhere, anywhere, pl.BlockSpec(memory_space=pltpu.VMEM)),
        scratch_shapes=[
            pltpu.VMEM((19,) + block, f32),
            pltpu.VMEM(block, jnp.int32),
            pltpu.VMEM(block, jnp.int32),
            pltpu.VMEM((3, 19, nx + 2, ny + 2 * ROWS, nz), f32),
            pltpu.VMEM((2, nx + 2 * RAD, ny + 2 * ROWS, nz), f32),
            pltpu.VMEM((4,) + block, f32),
            pltpu.VMEM(block, f32),
            pltpu.VMEM(block, f32),
            pltpu.VMEM((19,) + block, f32),
            pltpu.VMEM(block, f32),
            pltpu.VMEM((3, 2, 5, ny, nz), f32),
            pltpu.VMEM((3, 2, 5, ny, nz), f32),
            pltpu.VMEM((3, 2, 5, nx, nz), f32),
            pltpu.VMEM((3, 2, 5, nx, nz), f32),
            pltpu.VMEM((3, 4, 1, nz), f32),
            pltpu.VMEM((3, 4, 1, nz), f32),
            pltpu.VMEM((sizes[1], 2 * REG, nz), f32),
            pltpu.VMEM((sizes[0], 2 * REG, nz), f32),
            pltpu.SemaphoreType.DMA((7,)),
            pltpu.SemaphoreType.DMA((5, 8)),
            pltpu.SemaphoreType.DMA((5, 8)),
            pltpu.SemaphoreType.DMA((2, most)),
            pltpu.SemaphoreType.DMA((2, most)),
        ],
        compiler_params=pltpu.CompilerParams(
            collective_id=0, has_side_effects=True, vmem_limit_bytes=60 * 1024 * 1024
        ),
        name="lattice_adjoint",
    )(forward_pops, later_adjoint, design, node_type, region)
    adjoint, sensitivity, objective, volumes = pl.pallas_call(
        finish,
        out_shape=(
            jax.ShapeDtypeStruct((19,) + block, f32),
            jax.ShapeDtypeStruct(block, f32),
            jax.ShapeDtypeStruct((1,), f32),
            jax.ShapeDtypeStruct((REG,), f32),
        ),
        in_specs=[anywhere] * 3,
        out_specs=(anywhere, anywhere, scalars, scalars),
        scratch_shapes=[
            pltpu.VMEM((2 * REG, nz), f32),
            pltpu.VMEM((19,) + block, f32),
            pltpu.VMEM(block, f32),
            pltpu.SemaphoreType.DMA((41,)),
        ],
        compiler_params=pltpu.CompilerParams(vmem_limit_bytes=60 * 1024 * 1024),
        name="place_results",
    )(adjoint, sensitivity, stats)
    return adjoint, sensitivity, objective.reshape(()), volumes


def solution(mesh):
    sizes = (mesh.shape["gx"], mesh.shape["gy"])
    in_specs = (
        P(None, "gx", "gy", None),
        P(None, "gx", "gy", None),
        P("gx", "gy", None),
        P("gx", "gy", None),
        P("gx", "gy", None),
    )
    out_specs = (P(None, "gx", "gy", None), P("gx", "gy", None), P(), P())
    return jax.shard_map(
        functools.partial(per_device, sizes),
        mesh=mesh,
        in_specs=in_specs,
        out_specs=out_specs,
        check_vma=False,
    )
```

```python
import functools
import math

import jax
import jax.numpy as jnp
from jax import lax
from jax.experimental import pallas as pl
from jax.experimental.pallas import tpu as pltpu
from jax.sharding import PartitionSpec as P

RAD = 3
REG = 8
MESH = pl.DeviceIdType.MESH

VELOCITY = [
    (0, 0, 0),
    (1, 0, 0),
    (-1, 0, 0),
    (0, 1, 0),
    (0, -1, 0),
    (0, 0, 1),
    (0, 0, -1),
    (1, 1, 0),
    (-1, -1, 0),
    (1, -1, 0),
    (-1, 1, 0),
    (1, 0, 1),
    (-1, 0, -1),
    (1, 0, -1),
    (-1, 0, 1),
    (0, 1, 1),
    (0, -1, -1),
    (0, 1, -1),
    (0, -1, 1),
]
W0, W1, W2 = 1.0 / 3.0, 1.0 / 18.0, 1.0 / 36.0
PAIRS = [1, 3, 5, 7, 9, 11, 13, 15, 17]
OPPOSITE = [0, 2, 1, 4, 3, 6, 5, 8, 7, 10, 9, 12, 11, 14, 13, 16, 15, 18, 17]
RELAXATION = 1.0 / 0.6
BRINKMAN = 0.9

DIRS = [(1, 0), (-1, 0), (0, 1), (0, -1), (1, 1), (-1, -1), (1, -1), (-1, 1)]
ALONG_Y = [2, 3]
ACROSS_X = [0, 1, 4, 5, 6, 7]
ROWS = 8
POST, LATER, MIDDLE = 0, 1, 2
DESIGN, RAW = 3, 4


def weight(a, b, c):
    return max(RAD + 1 - math.sqrt(a * a + b * b + c * c), 0.0)


def crossing(direction, sign):
    return [
        i
        for i in range(19)
        if all(
            direction[a] == 0 or sign * VELOCITY[i][a] == direction[a] for a in range(2)
        )
    ]


def lanes(shape):
    return lax.broadcasted_iota(jnp.int32, shape, len(shape) - 1)


def shifted(value, offset):
    if offset == 0:
        return value
    depth = value.shape[-1]
    z = lanes(value.shape)
    rolled = pltpu.roll(value, (-offset) % depth, value.ndim - 1)
    inside = z < depth - offset if offset > 0 else z >= -offset
    return jnp.where(inside, rolled, 0.0)


def inverse_norm(shape):
    depth = shape[-1]
    z = lanes(shape)
    span = range(-RAD, RAD + 1)
    norm = jnp.zeros(shape, jnp.float32)
    for c in span:
        layer = sum(weight(a, b, c) for a in span for b in span)
        inside = (z + c >= 0) & (z + c < depth)
        norm = norm + jnp.where(inside, layer, 0.0)
    return 1.0 / norm


def filter_taps(field, x, y):
    classes = {}
    for a in range(-RAD, RAD + 1):
        for b in range(-RAD, RAD + 1):
            if weight(a, b, 0) > 0:
                value = field[x + RAD + a, ROWS + y + b : 2 * ROWS + y + b, :]
                key = a * a + b * b
                classes[key] = classes[key] + value if key in classes else value
    result = None
    for c in range(RAD + 1):
        layer = None
        for key, value in classes.items():
            w = max(RAD + 1 - math.sqrt(key + c * c), 0.0)
            if w > 0:
                layer = w * value if layer is None else layer + w * value
        if c == 0:
            result = layer
        else:
            result = result + shifted(layer, c) + shifted(layer, -c)
    return result


def pairs_of(p):
    return (
        {i: p[i] + p[i + 1] for i in PAIRS},
        {i: p[i] - p[i + 1] for i in PAIRS},
    )


def moments(p):
    even, odd = pairs_of(p)
    density = p[0] + (
        ((even[1] + even[3]) + (even[5] + even[7]))
        + ((even[9] + even[11]) + (even[13] + (even[15] + even[17])))
    )
    momenta = [
        (odd[1] + odd[7]) + (odd[9] + (odd[11] + odd[13])),
        (odd[3] + odd[7]) + (odd[15] + odd[17] - odd[9]),
        (odd[5] + odd[11]) + (odd[15] - odd[13] - odd[17]),
    ]
    return density, momenta


def along(i, u):
    total = None
    for a in range(3):
        if VELOCITY[i][a] != 0:
            if total is None:
                total = u[a]
            elif VELOCITY[i][a] > 0:
                total = total + u[a]
            else:
                total = total - u[a]
    return total


def rates(kind):
    return jnp.where(kind <= 1, RELAXATION, 1.0)


def collide(p, density, plain, kind, factor):
    u = [factor * v for v in plain]
    base = 1.0 - 1.5 * (u[0] * u[0] + u[1] * u[1] + u[2] * u[2])
    omega = rates(kind)
    keep = 1.0 - omega
    wall = kind == 2
    scale = omega * density
    scale1 = W1 * scale
    scale2 = W2 * scale
    out = [None] * 19
    out[0] = jnp.where(wall, p[0], keep * p[0] + (W0 * scale) * base)
    for i in PAIRS:
        c_u = along(i, u)
        s = scale1 if i < 7 else scale2
        even = s * (base + 4.5 * c_u * c_u)
        odd = s * (3.0 * c_u)
        out[i] = jnp.where(wall, p[i + 1], keep * p[i] + (even + odd))
        out[i + 1] = jnp.where(wall, p[i], keep * p[i + 1] + (even - odd))
    return out


def adjoint_parts(m, plain, factor):
    u = [factor * v for v in plain]
    even, odd = pairs_of(m)
    total = W0 * m[0] + W1 * (even[1] + even[3] + even[5])
    e79, e1113, e1517 = even[7] + even[9], even[11] + even[13], even[15] + even[17]
    total = total + W2 * (e79 + e1113 + e1517)
    first = [
        W1 * odd[1] + W2 * ((odd[7] + odd[9]) + (odd[11] + odd[13])),
        W1 * odd[3] + W2 * ((odd[7] - odd[9]) + (odd[15] + odd[17])),
        W1 * odd[5] + W2 * ((odd[11] - odd[13]) + (odd[15] - odd[17])),
    ]
    xx = W1 * even[1] + W2 * (e79 + e1113)
    yy = W1 * even[3] + W2 * (e79 + e1517)
    zz = W1 * even[5] + W2 * (e1113 + e1517)
    xy = W2 * (even[7] - even[9])
    xz = W2 * (even[11] - even[13])
    yz = W2 * (even[15] - even[17])
    second = [
        xx * u[0] + xy * u[1] + xz * u[2],
        xy * u[0] + yy * u[1] + yz * u[2],
        xz * u[0] + yz * u[1] + zz * u[2],
    ]

    def dot(p, q):
        return p[0] * q[0] + p[1] * q[1] + p[2] * q[2]

    scalar = total * (1.0 - 1.5 * dot(u, u)) + 3.0 * dot(u, first) + 4.5 * dot(u, second)
    vector = [3.0 * first[a] + 9.0 * second[a] - 3.0 * (u[a] * total) for a in range(3)]
    return scalar - dot(vector, u), vector


def adjoint_back(m, rest, vector, kind, factor):
    omega = rates(kind)
    keep = 1.0 - omega
    wall = kind == 2
    rest = omega * rest
    scale = omega * factor
    turned = [scale * v for v in vector]
    out = [None] * 19
    out[0] = jnp.where(wall, m[0], keep * m[0] + rest)
    for i in PAIRS:
        c_v = along(i, turned)
        out[i] = jnp.where(wall, m[i + 1], keep * m[i] + (rest + c_v))
        out[i + 1] = jnp.where(wall, m[i], keep * m[i + 1] + (rest - c_v))
    return out


def gradient(vector, density, plain, kind):
    inner = vector[0] * plain[0] + vector[1] * plain[1] + vector[2] * plain[2]
    return jnp.where(kind == 2, 0.0, rates(kind) * density * inner)


def kernel(
    sizes,
    forward_hbm,
    later_hbm,
    design_hbm,
    kind_hbm,
    region_hbm,
    adjoint_hbm,
    sensitivity_hbm,
    stats_ref,
    forward,
    kind,
    region,
    pops,
    fields,
    macro,
    factors,
    grads,
    result,
    smooth,
    x_send,
    x_recv,
    y_send,
    y_recv,
    c_send,
    c_recv,
    stat_y,
    stat_x,
    load_sem,
    send_sem,
    recv_sem,
    sum_send,
    sum_recv,
):
    count_x, count_y = sizes
    nx, ny = kind.shape[0], kind.shape[1]
    me_x, me_y = lax.axis_index("gx"), lax.axis_index("gy")
    halves = range(0, ny, ROWS)

    def device(dx, dy):
        return (
            lax.rem(me_x + dx + count_x, count_x),
            lax.rem(me_y + dy + count_y, count_y),
        )

    def rim_planes(body, carry):
        return lax.fori_loop(0, 2, lambda k, c: body(k * (nx - 1), c), carry)

    def inner_planes(body, carry):
        return lax.fori_loop(1, nx - 1, body, carry)

    inner = (pl.ds(1, nx), pl.ds(ROWS, ny))
    loads = [
        pltpu.make_async_copy(
            design_hbm, fields.at[0, pl.ds(RAD, nx), pl.ds(ROWS, ny)], load_sem.at[0]
        ),
        pltpu.make_async_copy(later_hbm, pops.at[LATER, :, inner[0], inner[1]], load_sem.at[1]),
        pltpu.make_async_copy(forward_hbm, forward, load_sem.at[2]),
        pltpu.make_async_copy(kind_hbm, kind, load_sem.at[3]),
        pltpu.make_async_copy(region_hbm, region, load_sem.at[4]),
    ]
    for load in loads:
        load.start()

    partners = {((dx + count_x) % count_x, (dy + count_y) % count_y) for dx, dy in DIRS}
    partners |= {(0, k) for k in range(1, count_y)} | {(k, 0) for k in range(1, count_x)}
    barrier = pltpu.get_barrier_semaphore()
    for dx, dy in sorted(partners):
        pl.semaphore_signal(barrier, inc=1, device_id=device(dx, dy), device_id_type=MESH)
    loads[0].wait()
    pl.semaphore_wait(barrier, len(partners))

    def field_copies(slot, exchange):
        copies = []
        for j, (dx, dy) in enumerate(DIRS):
            width = nx if dx == 0 else RAD
            source_x = {0: RAD, 1: nx, -1: RAD}[dx]
            target_x = {0: RAD, 1: 0, -1: nx + RAD}[dx]
            height = ny if dy == 0 else ROWS
            source_y = {0: ROWS, 1: ny, -1: ROWS}[dy]
            target_y = {0: ROWS, 1: 0, -1: ny + ROWS}[dy]
            copies.append(
                pltpu.make_async_remote_copy(
                    src_ref=fields.at[slot, pl.ds(source_x, width), pl.ds(source_y, height)],
                    dst_ref=fields.at[slot, pl.ds(target_x, width), pl.ds(target_y, height)],
                    send_sem=send_sem.at[exchange, j],
                    recv_sem=recv_sem.at[exchange, j],
                    device_id=device(dx, dy),
                    device_id_type=MESH,
                )
            )
        return copies

    def pops_copies(slot):
        copies = []
        for j, direction in enumerate(DIRS):
            if direction[1] == 0:
                source, target, k = x_send, x_recv, j
            elif direction[0] == 0:
                source, target, k = y_send, y_recv, j - 2
            else:
                source, target, k = c_send, c_recv, j - 4
            copies.append(
                pltpu.make_async_remote_copy(
                    src_ref=source.at[slot, k],
                    dst_ref=target.at[slot, k],
                    send_sem=send_sem.at[slot, j],
                    recv_sem=recv_sem.at[slot, j],
                    device_id=device(*direction),
                    device_id_type=MESH,
                )
            )
        return copies

    def send_pops(slot, sign, copies, which):
        for j in which:
            dx, dy = DIRS[j]
            x = nx if dx == 1 else 1
            y = ROWS + ny - 1 if dy == 1 else ROWS
            for k, i in enumerate(crossing((dx, dy), sign)):
                if dy == 0:
                    x_send[slot, j, k] = pops[slot, i, x, ROWS : ROWS + ny, :]
                elif dx == 0:
                    for row in range(nx):
                        y_send[slot, j - 2, k, row : row + 1, :] = pops[
                            slot, i, row + 1, y : y + 1, :
                        ]
                else:
                    c_send[slot, j - 4] = pops[slot, i, x, y : y + 1, :]
            copies[j].start()

    def take_pops(slot, sign, copies, which):
        for j in which:
            dx, dy = DIRS[j]
            copies[j].wait_recv()
            x = 0 if dx == 1 else nx + 1
            y = ROWS - 1 if dy == 1 else ROWS + ny
            for k, i in enumerate(crossing((dx, dy), sign)):
                if dy == 0:
                    pops[slot, i, x, ROWS : ROWS + ny, :] = x_recv[slot, j, k]
                elif dx == 0:
                    for row in range(nx):
                        pops[slot, i, row + 1, y : y + 1, :] = y_recv[
                            slot, j - 2, k, row : row + 1, :
                        ]
                else:
                    pops[slot, i, x, y : y + 1, :] = c_recv[slot, j - 4]

    def pick(slot, i, x, y, sign):
        cx, cy, cz = (sign * c for c in VELOCITY[i])
        value = pops[slot, i, x + 1 + cx, ROWS + y + cy : 2 * ROWS + y + cy, :]
        return shifted(value, cz)

    design_copies = field_copies(0, DESIGN)
    for copy in design_copies:
        copy.start()
    loads[1].wait()
    later_copies = pops_copies(LATER)
    send_pops(LATER, -1, later_copies, ACROSS_X + ALONG_Y)
    for load in loads[2:]:
        load.wait()

    def macroscopic(x, carry):
        for y in halves:
            density, momenta = moments([forward[i, x, y : y + ROWS, :] for i in range(19)])
            inverse = 1.0 / density
            macro[0, x, y : y + ROWS, :] = density
            for a in range(3):
                macro[a + 1, x, y : y + ROWS, :] = momenta[a] * inverse
        return carry

    lax.fori_loop(0, nx, macroscopic, 0)
    inv_norm = inverse_norm((ROWS, kind.shape[2]))
    for copy in design_copies:
        copy.wait_recv()

    def first_step(x, sums):
        sums = list(sums)
        for y in halves:
            rows = slice(y, y + ROWS)
            kinds = kind[x, rows, :]
            design_cell = kinds == 1
            filtered = filter_taps(fields.at[0], x, y) * inv_norm
            factor = jnp.where(design_cell, 1.0 - BRINKMAN * (1.0 - filtered), 1.0)
            factors[x, rows, :] = factor
            regions = region[x, rows, :]
            inside = jnp.where(design_cell, filtered, 0.0)
            for r in range(REG):
                sums[r] = sums[r] + jnp.where(regions == r, inside, 0.0)
            post = collide(
                [forward[i, x, rows, :] for i in range(19)],
                macro[0, x, rows, :],
                [macro[a + 1, x, rows, :] for a in range(3)],
                kinds,
                factor,
            )
            for i in range(19):
                pops[POST, i, x + 1, ROWS + y : 2 * ROWS + y, :] = post[i]
        return tuple(sums)

    zero = jnp.zeros((ROWS, kind.shape[2]), jnp.float32)
    post_copies = pops_copies(POST)
    volumes = rim_planes(first_step, (zero,) * REG)
    send_pops(POST, 1, post_copies, ACROSS_X)
    volumes = inner_planes(first_step, volumes)
    send_pops(POST, 1, post_copies, ALONG_Y)
    take_pops(LATER, -1, later_copies, ALONG_Y + ACROSS_X)
    take_pops(POST, 1, post_copies, ALONG_Y)

    def middle_step(x, total):
        for y in halves:
            rows = slice(y, y + ROWS)
            kinds = kind[x, rows, :]
            factor = factors[x, rows, :]
            density, momenta = moments([pick(POST, i, x, y, -1) for i in range(19)])
            outlet = kinds == 4
            total = total + jnp.where(outlet, momenta[0], 0.0)
            inverse = 1.0 / density
            plain = [m * inverse for m in momenta]
            incoming = [pick(LATER, i, x, y, 1) for i in range(19)]
            rest, vector = adjoint_parts(incoming, plain, factor)
            grads[x, rows, :] = gradient(vector, density, plain, kinds)
            middle = adjoint_back(incoming, rest, vector, kinds, factor)
            source = jnp.where(outlet, 1.0, 0.0)
            for i in range(19):
                value = middle[i]
                if VELOCITY[i][0] == 1:
                    value = value + source
                elif VELOCITY[i][0] == -1:
                    value = value - source
                pops[MIDDLE, i, x + 1, ROWS + y : 2 * ROWS + y, :] = value
        return total

    objective = inner_planes(middle_step, zero)
    take_pops(POST, 1, post_copies, ACROSS_X)
    objective = rim_planes(middle_step, objective)
    middle_copies = pops_copies(MIDDLE)
    send_pops(MIDDLE, -1, middle_copies, ACROSS_X + ALONG_Y)

    def spread(stat, count, me, sem, place):
        copies = []
        for k in range(1, count):
            copies.append(
                pltpu.make_async_remote_copy(
                    src_ref=stat.at[me],
                    dst_ref=stat.at[me],
                    send_sem=sum_send.at[sem, k],
                    recv_sem=sum_recv.at[sem, k],
                    device_id=place(k),
                    device_id_type=MESH,
                )
            )
        for copy in copies:
            copy.start()
        return copies

    for r in range(REG):
        stat_y[me_y, r : r + 1, :] = jnp.sum(volumes[r], axis=0, keepdims=True)
    stat_y[me_y, REG : REG + 1, :] = jnp.sum(objective, axis=0, keepdims=True)
    stat_y[me_y, REG + 1 :, :] = jnp.zeros((REG - 1, zero.shape[1]), jnp.float32)
    sums_y = spread(stat_y, count_y, me_y, 0, lambda k: device(0, k))
    take_pops(MIDDLE, -1, middle_copies, ALONG_Y)

    def second_step(x, carry):
        for y in halves:
            rows = slice(y, y + ROWS)
            kinds = kind[x, rows, :]
            factor = factors[x, rows, :]
            density = macro[0, x, rows, :]
            plain = [macro[a + 1, x, rows, :] for a in range(3)]
            incoming = [pick(MIDDLE, i, x, y, 1) for i in range(19)]
            rest, vector = adjoint_parts(incoming, plain, factor)
            grad = grads[x, rows, :] + gradient(vector, density, plain, kinds)
            raw = jnp.where(kinds == 1, BRINKMAN * grad, 0.0) * inv_norm
            fields[1, x + RAD, ROWS + y : 2 * ROWS + y, :] = raw
            back = adjoint_back(incoming, rest, vector, kinds, factor)
            for i in range(19):
                result[i, x, rows, :] = back[i]
        return carry

    inner_planes(second_step, 0)
    for copy in sums_y:
        copy.wait()
    subtotal = stat_y[0]
    for k in range(1, count_y):
        subtotal = subtotal + stat_y[k]
    stat_x[me_x] = subtotal
    sums_x = spread(stat_x, count_x, me_x, 1, lambda k: device(k, 0))
    take_pops(MIDDLE, -1, middle_copies, ACROSS_X)
    rim_planes(second_step, 0)
    raw_copies = field_copies(1, RAW)
    for copy in raw_copies:
        copy.start()
    store = pltpu.make_async_copy(result, adjoint_hbm, load_sem.at[5])
    store.start()

    for copy in raw_copies:
        copy.wait_recv()

    def last_step(x, carry):
        for y in halves:
            smooth[x, y : y + ROWS, :] = filter_taps(fields.at[1], x, y)
        return carry

    lax.fori_loop(0, nx, last_step, 0)
    store_smooth = pltpu.make_async_copy(smooth, sensitivity_hbm, load_sem.at[6])
    store_smooth.start()
    for copy in sums_x:
        copy.wait()
    total = stat_x[0]
    for k in range(1, count_x):
        total = total + stat_x[k]
    stats_ref[...] = total
    for copies in (design_copies, later_copies, post_copies, middle_copies, raw_copies):
        for copy in copies:
            copy.wait_send()
    store.wait()
    store_smooth.wait()


def finish(
    adjoint_in,
    sensitivity_in,
    stats_in,
    adjoint_out,
    sensitivity_out,
    objective_ref,
    volumes_ref,
    stats,
    held,
    smooth,
    sem,
):
    load = pltpu.make_async_copy(stats_in, stats, sem.at[0])
    load.start()
    ways = [(adjoint_in.at[i], held.at[i], adjoint_out.at[i]) for i in range(19)]
    ways.append((sensitivity_in, smooth, sensitivity_out))
    loads = [
        pltpu.make_async_copy(way[0], way[1], sem.at[1 + k])
        for k, way in enumerate(ways)
    ]
    copies = [
        pltpu.make_async_copy(way[1], way[2], sem.at[21 + k])
        for k, way in enumerate(ways)
    ]
    for copy in loads:
        copy.start()
    for arrival, copy in zip(loads, copies):
        arrival.wait()
        copy.start()
    load.wait()
    total = jnp.sum(stats[...], axis=1, keepdims=True)
    for r in range(REG):
        volumes_ref[r] = total[r, 0]
    objective_ref[0] = total[REG, 0]
    for copy in copies:
        copy.wait()


def per_device(sizes, forward_pops, later_adjoint, design, node_type, region):
    nx, ny, nz = design.shape
    f32 = jnp.float32
    anywhere = pl.BlockSpec(memory_space=pl.ANY)
    scalars = pl.BlockSpec(memory_space=pltpu.SMEM)
    block = (nx, ny, nz)
    most = max(sizes)
    adjoint, sensitivity, stats = pl.pallas_call(
        functools.partial(kernel, sizes),
        out_shape=(
            jax.ShapeDtypeStruct((19,) + block, f32),
            jax.ShapeDtypeStruct(block, f32),
            jax.ShapeDtypeStruct((2 * REG, nz), f32),
        ),
        in_specs=[anywhere] * 5,
        out_specs=(anywhere, anywhere, pl.BlockSpec(memory_space=pltpu.VMEM)),
        scratch_shapes=[
            pltpu.VMEM((19,) + block, f32),
            pltpu.VMEM(block, jnp.int32),
            pltpu.VMEM(block, jnp.int32),
            pltpu.VMEM((3, 19, nx + 2, ny + 2 * ROWS, nz), f32),
            pltpu.VMEM((2, nx + 2 * RAD, ny + 2 * ROWS, nz), f32),
            pltpu.VMEM((4,) + block, f32),
            pltpu.VMEM(block, f32),
            pltpu.VMEM(block, f32),
            pltpu.VMEM((19,) + block, f32),
            pltpu.VMEM(block, f32),
            pltpu.VMEM((3, 2, 5, ny, nz), f32),
            pltpu.VMEM((3, 2, 5, ny, nz), f32),
            pltpu.VMEM((3, 2, 5, nx, nz), f32),
            pltpu.VMEM((3, 2, 5, nx, nz), f32),
            pltpu.VMEM((3, 4, 1, nz), f32),
            pltpu.VMEM((3, 4, 1, nz), f32),
            pltpu.VMEM((sizes[1], 2 * REG, nz), f32),
            pltpu.VMEM((sizes[0], 2 * REG, nz), f32),
            pltpu.SemaphoreType.DMA((7,)),
            pltpu.SemaphoreType.DMA((5, 8)),
            pltpu.SemaphoreType.DMA((5, 8)),
            pltpu.SemaphoreType.DMA((2, most)),
            pltpu.SemaphoreType.DMA((2, most)),
        ],
        compiler_params=pltpu.CompilerParams(
            collective_id=0, has_side_effects=True, vmem_limit_bytes=60 * 1024 * 1024
        ),
        name="lattice_adjoint",
    )(forward_pops, later_adjoint, design, node_type, region)
    adjoint, sensitivity, objective, volumes = pl.pallas_call(
        finish,
        out_shape=(
            jax.ShapeDtypeStruct((19,) + block, f32),
            jax.ShapeDtypeStruct(block, f32),
            jax.ShapeDtypeStruct((1,), f32),
            jax.ShapeDtypeStruct((REG,), f32),
        ),
        in_specs=[anywhere] * 3,
        out_specs=(anywhere, anywhere, scalars, scalars),
        scratch_shapes=[
            pltpu.VMEM((2 * REG, nz), f32),
            pltpu.VMEM((19,) + block, f32),
            pltpu.VMEM(block, f32),
            pltpu.SemaphoreType.DMA((41,)),
        ],
        compiler_params=pltpu.CompilerParams(vmem_limit_bytes=60 * 1024 * 1024),
        name="place_results",
    )(adjoint, sensitivity, stats)
    return adjoint, sensitivity, objective.reshape(()), volumes


def solution(mesh):
    sizes = (mesh.shape["gx"], mesh.shape["gy"])
    in_specs = (
        P(None, "gx", "gy", None),
        P(None, "gx", "gy", None),
        P("gx", "gy", None),
        P("gx", "gy", None),
        P("gx", "gy", None),
    )
    out_specs = (P(None, "gx", "gy", None), P("gx", "gy", None), P(), P())
    return jax.shard_map(
        functools.partial(per_device, sizes),
        mesh=mesh,
        in_specs=in_specs,
        out_specs=out_specs,
        check_vma=False,
    )
```
